512 devices in a mesh: tm: 16 (over x, y), tile: 32 (over z, core).
Axes of the slice: x: 4, y: 4, z: 16, core: 2. Of those that a mesh axis runs over, the one named last changes fastest.
Arguments:
- haar_video: bfloat16 [64, 128, 6144], P('tm', 'tile'), may hold values from -6 to 6
- clip_lengths: int32 [16], replicated, may hold values from 1 to 8, 64 in all
- block_owner: int32 [16], replicated, may hold values from 0 to 15, each once
- spatial_in: bfloat16 [3, 3, 48, 128], replicated, may hold values from -0.3125 to 0.3125
- temporal_in: bfloat16 [3, 128, 128], replicated, may hold values from -0.3125 to 0.3125
- bias_in: float32 [128], replicated, may hold values from -4 to 4
- spatial_down: bfloat16 [3, 3, 128, 256], replicated, may hold values from -0.25 to 0.25
- temporal_down: bfloat16 [3, 256, 256], replicated, may hold values from -0.25 to 0.25
- bias_down: float32 [256], replicated, may hold values from -4 to 4
- spatial_out: bfloat16 [3, 3, 256, 256], replicated, may hold values from -0.1875 to 0.1875
- temporal_out: bfloat16 [3, 256, 256], replicated, may hold values from -0.25 to 0.25
- bias_out: float32 [256], replicated, may hold values from -3 to 3
Outputs:
- latents: bfloat16 [32, 64, 64, 256], P('tm', 'tile')
The draws below stay inside these ranges and needn't reach their ends.
Inputs may be any that keep to these rules, and one draw needn't show every extreme that they name: `clip_lengths`: the clip lengths sum to 64; the longest is exactly 8. `block_owner`: every tm index is named exactly once.
All inputs are finite; a program needn't handle non-finite values.
Results may differ from the reference program's by a relative error of at most 0.015.
Values may be sent and summed in bfloat16 or wider, within the bound.
A program may use at most 64 MiB of HBM per device.

```python
import math
import jax
import jax.numpy as jnp
import numpy as np
from jax import lax

CIN = 48
C1 = 128
C2 = 256
F_DEV = 4
COLS = 128
FRAMES = 64
ROWS = 128
CLIPS = 16
MOST = 8
N_TM = 16


def shard_levels(key, dims, cuts, smallest, top_value):
    loudness, own = 1.0, jax.random.fold_in(key, 6)
    for dim, parts in cuts:
        heights = jnp.exp(jax.random.uniform(jax.random.fold_in(own, dim), (parts,), jnp.float32, smallest / len(cuts), top_value / len(cuts)))
        loudness = loudness * jnp.repeat(heights, dims[dim] // parts).reshape([-1 if axis == dim else 1 for axis in range(len(dims))])
    return loudness


def split_up(count, total, limit, lean):
    loads = [(1 << 20) // math.isqrt(rank ** lean) + 1 for rank in range(2, count + 1)]
    spare, counts = total - limit - (count - 1), [1] * (count - 1)
    while spare > 0:
        movable = [i for i in range(count - 1) if counts[i] < limit]
        mass, left = sum([loads[i] for i in movable]), spare
        for i in movable:
            extra = min(limit - counts[i], max(1, left * loads[i] // mass), spare)
            counts[i] = counts[i] + extra
            spare = spare - extra
    return np.array([limit] + counts)


def ragged(rng, number_of, total, most, skew):
    if number_of == 2:
        one = jax.random.randint(rng, (), max(1, total - most), min(most, total - 1) + 1)
        return jnp.stack([one, total - one])
    lengths = jnp.asarray(split_up(number_of, total, most, skew), jnp.int32)
    twos = (number_of - 1) // 2
    giver, receiver = lengths[1:1 + 2 * twos:2], lengths[2:2 + 2 * twos:2]
    slack = jnp.minimum(giver - 1, most - receiver)
    passed = jax.random.randint(jax.random.fold_in(rng, 1), (twos,), 0, 1 << 20) % (slack + 1)
    lengths = lengths.at[1:1 + 2 * twos:2].set(giver - passed).at[2:2 + 2 * twos:2].set(receiver + passed)
    return lengths[jax.random.permutation(jax.random.fold_in(rng, 2), number_of)]


def normal_values(own_key, dims, deviation, bound, cuts=(), held_as=jnp.bfloat16):
    level = shard_levels(own_key, dims, cuts, -0.22, 0.18) if cuts else 1.0
    array = jax.random.normal(own_key, dims, jnp.float32) * deviation * level
    return jnp.minimum(jnp.maximum(array, -bound), bound).astype(held_as)


def setup_inputs(seed: int = 0) -> dict:
    streams_of = jax.random.split(jax.random.key(seed), 13)
    haar_video = normal_values(streams_of[0], (FRAMES, ROWS, COLS * CIN), 1.0, 6.0, ((0, 16), (1, 32)))
    clip_lengths = ragged(streams_of[1], CLIPS, FRAMES, MOST, 2).astype(jnp.int32)
    block_owner = jax.random.permutation(streams_of[2], N_TM).astype(jnp.int32)
    spatial_in = normal_values(streams_of[3], (3, 3, CIN, C1), (9 * CIN) ** -0.5, 0.3125)
    temporal_in = normal_values(streams_of[4], (3, C1, C1), (3 * C1) ** -0.5, 0.3125)
    bias_in = normal_values(streams_of[5], (C1,), 1.0, 4.0, (), jnp.float32)
    spatial_down = normal_values(streams_of[6], (3, 3, C1, C2), (4 * C1) ** -0.5, 0.25)
    temporal_down = normal_values(streams_of[7], (3, C2, C2), (2 * C2) ** -0.5, 0.25)
    bias_down = normal_values(streams_of[8], (C2,), 1.0, 4.0, (), jnp.float32)
    spatial_out = normal_values(streams_of[9], (3, 3, C2, C2), (4 * C2) ** -0.5, 0.1875)
    temporal_out = normal_values(streams_of[10], (3, C2, C2), (2 * C2) ** -0.5, 0.25)
    bias_out = normal_values(streams_of[11], (C2,), 0.5, 3.0, (), jnp.float32)
    return dict(haar_video=haar_video, clip_lengths=clip_lengths, block_owner=block_owner, spatial_in=spatial_in, temporal_in=temporal_in, bias_in=bias_in, spatial_down=spatial_down, temporal_down=temporal_down, bias_down=bias_down, spatial_out=spatial_out, temporal_out=temporal_out, bias_out=bias_out)


def clip_of(frame_ids, clip_lengths):
    clip_ends = jnp.cumsum(clip_lengths)
    return jnp.sum((clip_ends[None, :] <= frame_ids[:, None]).astype(jnp.int32), axis=1)


def tap_mask(key_frames, tap_frames, clip_lengths):
    tap_clips = clip_of(tap_frames.reshape(-1), clip_lengths).reshape(tap_frames.shape)
    same_clip = tap_clips == clip_of(key_frames, clip_lengths)[:, None]
    return jnp.where(same_clip & (tap_frames >= 0), 1.0, 0.0).astype(jnp.bfloat16)


def spatial_conv(row_extended, kernel, stride, out_rows, out_cols):
    pad_right = 1 if stride == 1 else 0
    padded = jnp.pad(row_extended, ((0, 0), (0, 0), (1, pad_right), (0, 0)))
    pieces = [padded[:, row_tap:row_tap + stride * out_rows:stride, col_tap:col_tap + stride * out_cols:stride]
              for row_tap in range(3) for col_tap in range(3)]
    patches = jnp.concatenate(pieces, axis=-1)
    flattened = jnp.dot(patches.reshape(-1, patches.shape[-1]), kernel.reshape(-1, kernel.shape[-1]),
                        preferred_element_type=jnp.float32)
    return flattened.reshape(patches.shape[:-1] + (kernel.shape[-1],))


def temporal_steps(extended, kernel, mask, out_count, stride, bias, activate):
    def one_step(frame_index):
        running = jnp.zeros(extended.shape[1:-1] + (kernel.shape[-1],), jnp.float32)
        mask_row = lax.dynamic_index_in_dim(mask, frame_index, 0, keepdims=False)
        for lag in range(3):
            one_frame = lax.dynamic_index_in_dim(extended, frame_index * stride + lag, 0, keepdims=False)
            one_frame = one_frame * mask_row[lag]
            tap_term = jnp.dot(one_frame.reshape(-1, one_frame.shape[-1]), kernel[lag],
                               preferred_element_type=jnp.float32)
            running = running + tap_term.reshape(running.shape)
        running = running + bias
        if activate:
            running = jax.nn.silu(running)
        return running.astype(jnp.bfloat16)
    return lax.map(one_step, jnp.arange(out_count, dtype=jnp.int32))


def reference(haar_video, clip_lengths, block_owner, spatial_in, temporal_in, bias_in, spatial_down,
              temporal_down, bias_down, spatial_out, temporal_out, bias_out):
    frames = haar_video.reshape(FRAMES, ROWS, COLS, CIN)
    lags = jnp.arange(3, dtype=jnp.int32)
    padded = jnp.pad(frames, ((0, 0), (1, 1), (0, 0), (0, 0)))
    spatial_one = lax.map(lambda one_frame: spatial_conv(one_frame[None], spatial_in, 1, ROWS, COLS)[0].astype(jnp.bfloat16), padded)
    frame_ids = jnp.arange(FRAMES, dtype=jnp.int32)
    first_mask = tap_mask(frame_ids, frame_ids[:, None] + lags[None, :] - 2, clip_lengths)
    extended = jnp.pad(spatial_one, ((2, 0), (0, 0), (0, 0), (0, 0)))
    hidden_one = temporal_steps(extended, temporal_in, first_mask, FRAMES, 1, bias_in, True)
    padded = jnp.pad(hidden_one, ((0, 0), (1, 0), (0, 0), (0, 0)))
    spatial_two = lax.map(lambda one_frame: spatial_conv(one_frame[None], spatial_down, 2, ROWS // 2, COLS // 2)[0].astype(jnp.bfloat16), padded)
    reduced_ids = jnp.arange(FRAMES // 2, dtype=jnp.int32)
    second_mask = tap_mask(2 * reduced_ids + 1, 2 * reduced_ids[:, None] + lags[None, :] - 1, clip_lengths)
    extended = jnp.pad(spatial_two, ((1, 0), (0, 0), (0, 0), (0, 0)))
    hidden_two = temporal_steps(extended, temporal_down, second_mask, FRAMES // 2, 2, bias_down, True)
    padded = jnp.pad(hidden_two, ((0, 0), (1, 1), (0, 0), (0, 0)))
    spatial_three = lax.map(lambda one_frame: spatial_conv(one_frame[None], spatial_out, 1, ROWS // 2, COLS // 2)[0].astype(jnp.bfloat16), padded)
    reduced_taps = reduced_ids[:, None] + lags[None, :] - 2
    third_mask = tap_mask(2 * reduced_ids + 1, 2 * reduced_taps + 1, clip_lengths)
    extended = jnp.pad(spatial_three, ((2, 0), (0, 0), (0, 0), (0, 0)))
    encoded = temporal_steps(extended, temporal_out, third_mask, FRAMES // 2, 1, bias_out, False)
    blocks = encoded.reshape((N_TM, F_DEV // 2) + encoded.shape[1:])
    slots = jnp.arange(N_TM, dtype=jnp.int32)
    source_of = jnp.sum(jnp.where(block_owner[None, :] == slots[:, None], slots[None, :], 0), axis=1)
    return blocks[source_of].reshape(encoded.shape)
```

```python
import functools

import jax
import jax.numpy as jnp
from jax import lax
from jax.experimental import pallas as pl
from jax.experimental.pallas import tpu as pltpu
from jax.sharding import PartitionSpec as P

MESH = pl.DeviceIdType.MESH
BF, F32 = jnp.bfloat16, jnp.float32

GROUPS = ((0, 0, 3), (1, 3, 3), (2, 6, 2), (3, 8, 3), (4, 11, 2))
PATCH = 768
STEP = 384


def iota(shape, dim):
    return lax.broadcasted_iota(jnp.int32, shape, dim)


def dot(a, b):
    return jnp.dot(a, b, preferred_element_type=F32)


def silu(v):
    return (0.5 * v) * (1.0 + jnp.tanh(0.5 * v))


def one_hot(row_key, col_key):
    return jnp.where(row_key == col_key, 1.0, 0.0).astype(BF)


def clip_of(frames, clip_ref, clips):
    total = jnp.zeros(frames.shape, jnp.int32)
    end = 0
    for k in range(clips):
        end = end + clip_ref[k]
        total = total + jnp.where(frames >= end, 1, 0)
    return total


def same_clip(key, tap, clip_ref, clips):
    same = clip_of(key, clip_ref, clips) == clip_of(tap, clip_ref, clips)
    return jnp.where(same & (tap >= 0), 1.0, 0.0)


def build_first_weights(win_ref, w1_ref):
    for g, (window, first, count) in enumerate(GROUPS):
        w1_ref[g] = jnp.zeros(w1_ref.shape[1:], BF)
        for a in range(3):
            for b in range(3):
                for n in range(count):
                    at = a * 256 + 48 * (first + n + b) - 128 * window
                    w1_ref[g, at : at + 48, n * 128 : (n + 1) * 128] = win_ref[a, b]


def build_temporal_weights(tin_ref, wt_ref):
    zero = jnp.zeros((128, 128), BF)
    blocks = (((0, None), (None, 2)), ((1, 0), (2, 1)))
    for part in range(2):
        for i in range(2):
            for j in range(2):
                k = blocks[part][i][j]
                wt_ref[part, i * 128 : (i + 1) * 128, j * 128 : (j + 1) * 128] = (
                    zero if k is None else tin_ref[k]
                )


def spread(recv_ref, x_ref, rel):
    row, col = iota((256, 256), 0), iota((256, 256), 1)
    perm = one_hot((row % 16) * 16 + ((row // 16) % 4) * 4 + row // 64, col)
    for half in range(2):
        lanes = slice(half * 384, half * 384 + 384)
        block = recv_ref[rel, :, :, lanes].reshape(256, 384)
        x_ref[4 * rel : 4 * rel + 4, :, :, lanes] = (
            dot(perm, block).astype(BF).reshape(4, 4, 16, 384)
        )


def first_spatial(x_ref, w1_ref, lt_ref, masks, row0, rows):
    for g, (window, first, count) in enumerate(GROUPS):
        lanes = slice(128 * window, 128 * window + 256)
        taps = [
            x_ref[pl.ds(row0 + a, rows), :, :, lanes].reshape(rows * 64, 256)
            for a in range(3)
        ]
        made = dot(jnp.concatenate(taps, axis=1), w1_ref[g, :, : count * 128])
        for n in range(count):
            s = made[:, n * 128 : (n + 1) * 128].reshape(rows, 4, 16, 128)
            late = s[:, 2:4].reshape(rows * 32, 128)
            late = pltpu.roll(late, 1, 0).reshape(rows, 2, 16, 128)
            at = (first + n, pl.ds(row0, rows))
            left, right = slice(0, 128), slice(128, 256)
            lt_ref[(0,) + at + (0, slice(None), left)] = (late[:, 0] * masks[0]).astype(BF)
            lt_ref[(0,) + at + (0, slice(None), right)] = s[:, 1].astype(BF)
            lt_ref[(1,) + at + (0, slice(None), left)] = (late[:, 1] * masks[1]).astype(BF)
            lt_ref[(1,) + at + (0, slice(None), right)] = s[:, 0].astype(BF)
            lt_ref[(0,) + at + (1, slice(None), left)] = (s[:, 0] * masks[2]).astype(BF)
            lt_ref[(0,) + at + (1, slice(None), right)] = s[:, 3].astype(BF)
            lt_ref[(1,) + at + (1, slice(None), left)] = (s[:, 1] * masks[3]).astype(BF)
            lt_ref[(1,) + at + (1, slice(None), right)] = s[:, 2].astype(BF)


def first_temporal(lt_ref, wt_ref, h1_ref, bias, pair_mask, col):
    one = dot(lt_ref[0, col].reshape(288, 256), wt_ref[0]).reshape(9, 2, 16, 256)
    two = dot(lt_ref[1, col].reshape(288, 256), wt_ref[1]).reshape(9, 2, 16, 256)
    early = one[..., :128] + two[..., :128] + bias
    late = one[..., 128:] + two[..., 128:] * pair_mask[None] + bias
    h1_ref[col % 2, col // 2, :, :, 0] = silu(early).astype(BF)
    h1_ref[col % 2, col // 2, :, :, 1] = silu(late).astype(BF)


def second(h1_ref, down_ref, tdown_ref, h2_ref, bias, masks, q):
    taps = [
        h1_ref[b % 2, b // 2 : b // 2 + 6, 2 * q + a].reshape(384, 128)
        for a in range(3)
        for b in range(3)
    ]
    s = dot(jnp.concatenate(taps, axis=1), down_ref[...].reshape(1152, 256))
    s = s.reshape(6, 2, 2, 16, 256)
    before = pltpu.roll(s[:, 1, 1].reshape(96, 256), 1, 0).reshape(6, 1, 16, 256)
    k0 = jnp.concatenate([before, s[:, 0:1, 1]], axis=1) * masks[0]
    k1 = s[:, :, 0] * masks[1]
    k2 = s[:, :, 1]
    taps = jnp.concatenate(
        [k.astype(BF).reshape(192, 256) for k in (k0, k1, k2)], axis=1
    )
    made = dot(taps, tdown_ref[...].reshape(768, 256)) + bias
    h2_ref[q] = silu(made).astype(BF).reshape(6, 2, 16, 256)


def third(h2_ref, wout_ref, tout_ref, bias, masks):
    taps = [
        h2_ref[a : a + 2, b : b + 4].reshape(256, 256) for a in range(3) for b in range(3)
    ]
    s = dot(jnp.concatenate(taps, axis=1), wout_ref[...].reshape(2304, 256))
    before = pltpu.roll(s, 1, 0).reshape(8, 2, 16, 256)
    s = s.reshape(8, 2, 16, 256)
    k0 = before * masks[0]
    k1 = jnp.concatenate([before[:, 1:2], s[:, 0:1]], axis=1) * masks[1]
    taps = jnp.concatenate([k.astype(BF).reshape(256, 256) for k in (k0, k1, s)], axis=1)
    return (dot(taps, tout_ref[...].reshape(768, 256)) + bias).astype(BF)


def local_part(
    clips, at_left, at_right, at_top, at_bottom, clip_ref, recv_ref, x_ref, w1_ref, lt_ref,
    wt_ref, h1_ref, h2_ref, down_ref, tdown_ref, wout_ref, tout_ref, bin_ref, bdown_ref, bout_ref,
):
    for rel in range(3):
        spread(recv_ref, x_ref, rel)
    base = 4 * iota((16, 128), 0)
    check = functools.partial(same_clip, clip_ref=clip_ref, clips=clips)
    masks = [check(base, base - 2), check(base, base - 1), check(base + 2, base), check(base + 2, base + 1)]
    pair_mask = jnp.stack([check(base + 1, base), check(base + 3, base + 2)])

    def rows_of(i, carry):
        first_spatial(x_ref, w1_ref, lt_ref, masks, 3 * i, 3)
        return carry

    lax.fori_loop(0, 3, rows_of, 0)
    bias_in = bin_ref[...]

    def column(i, carry):
        first_temporal(lt_ref, wt_ref, h1_ref, bias_in, pair_mask, i)
        return carry

    lax.fori_loop(0, 13, column, 0)

    @pl.when(at_top)
    def _():
        h1_ref[:, :, 2] = jnp.zeros((2, 7, 2, 2, 16, 128), BF)

    @pl.when(at_left)
    def _():
        h1_ref[0, 1] = jnp.zeros((9, 2, 2, 16, 128), BF)

    base = 4 * iota((2, 16, 256), 1) + 2 * iota((2, 16, 256), 0)
    masks = [check(base + 1, base - 1), check(base + 1, base)]
    bias_down = bdown_ref[...]

    def reduced_row(i, carry):
        second(h1_ref, down_ref, tdown_ref, h2_ref, bias_down, masks, i)
        return carry

    lax.fori_loop(0, 4, reduced_row, 0)

    @pl.when(at_top)
    def _():
        h2_ref[0] = jnp.zeros((6, 2, 16, 256), BF)

    @pl.when(at_bottom)
    def _():
        h2_ref[3] = jnp.zeros((6, 2, 16, 256), BF)

    @pl.when(at_left)
    def _():
        h2_ref[:, 0] = jnp.zeros((4, 2, 16, 256), BF)

    @pl.when(at_right)
    def _():
        h2_ref[:, 5] = jnp.zeros((4, 2, 16, 256), BF)

    masks = [check(base + 1, base - 3), check(base + 1, base - 1)]
    return third(h2_ref, wout_ref, tout_ref, bout_ref[...], masks)


def kernel(
    clips,
    x_ref, clip_ref, owner_ref, win_ref, tin_ref, bin_ref, down_hbm, tdown_hbm, bdown_ref, wout_hbm, tout_hbm, bout_ref,
    out_ref,
    xpad, recv, xs, w1, lt, wt, h1, h2, down, tdown, wout, tout, parts, landed,
    weight_sem, own_sem, send_sem, recv_sem, fsend_sem, frecv_sem, send2_sem, recv2_sem,
):
    me, row = lax.axis_index("tm"), lax.axis_index("tile")
    n, n_rows = lax.axis_size("tm"), lax.axis_size("tile")
    at_top, at_bottom = row == 0, row == n_rows - 1
    barrier = pltpu.get_barrier_semaphore()
    for k in range(1, n):
        pl.semaphore_signal(barrier, inc=1, device_id={"tm": lax.rem(me + k, n)}, device_id_type=MESH)

    @pl.when(jnp.logical_not(at_top))
    def _():
        pl.semaphore_signal(barrier, inc=1, device_id={"tile": row - 1}, device_id_type=MESH)

    @pl.when(jnp.logical_not(at_bottom))
    def _():
        pl.semaphore_signal(barrier, inc=1, device_id={"tile": row + 1}, device_id_type=MESH)

    loads = [
        pltpu.make_async_copy(source, target, weight_sem.at[i])
        for i, (source, target) in enumerate(
            ((down_hbm, down), (tdown_hbm, tdown), (wout_hbm, wout), (tout_hbm, tout))
        )
    ]
    for load in loads:
        load.start()
    mine = jnp.concatenate([x_ref[f].astype(F32) for f in range(4)], axis=0)
    side = jnp.zeros((16, 192), F32)
    xpad[...] = jnp.concatenate([side, mine, side], axis=1).astype(BF)
    pl.semaphore_wait(barrier, n - 1 + jnp.where(at_top, 0, 1) + jnp.where(at_bottom, 0, 1))

    def patch(who):
        return xpad.at[:, pl.ds(pl.multiple_of(who * STEP, 128), PATCH)]

    def sent(k):
        to = lax.rem(me + k, n)
        return pltpu.make_async_remote_copy(
            src_ref=patch(to), dst_ref=recv.at[1, me], send_sem=send_sem.at[k], recv_sem=recv_sem.at[me],
            device_id={"tm": to}, device_id_type=MESH,
        )

    def arriving(k):
        source = lax.rem(me - k + n, n)
        return pltpu.make_async_remote_copy(
            src_ref=patch(me), dst_ref=recv.at[1, source], send_sem=send_sem.at[k], recv_sem=recv_sem.at[source],
            device_id={"tm": source}, device_id_type=MESH,
        )

    def passed(source, down_way):
        way, to = (0, row + 1) if down_way else (1, row - 1)
        return pltpu.make_async_remote_copy(
            src_ref=recv.at[1, source], dst_ref=recv.at[2 * way, source], send_sem=fsend_sem.at[way, source],
            recv_sem=frecv_sem.at[way, source], device_id={"tile": to}, device_id_type=MESH,
        )

    def pass_on(source):
        @pl.when(jnp.logical_not(at_bottom))
        def _():
            passed(source, True).start()

        @pl.when(jnp.logical_not(at_top))
        def _():
            passed(source, False).start()

    def start_send(k, carry):
        sent(k).start()
        return carry

    lax.fori_loop(1, n, start_send, 0)
    own = pltpu.make_async_copy(patch(me), recv.at[1, me], own_sem)
    own.start()
    own.wait()
    pass_on(me)
    build_first_weights(win_ref, w1)
    build_temporal_weights(tin_ref, wt)

    @pl.when(at_top)
    def _():
        recv[0] = jnp.zeros(recv.shape[1:], BF)

    @pl.when(at_bottom)
    def _():
        recv[2] = jnp.zeros(recv.shape[1:], BF)

    def relay(k, carry):
        arriving(k).wait_recv()
        pass_on(lax.rem(me - k + n, n))
        return carry

    lax.fori_loop(1, n, relay, 0)

    def settle(k, carry):
        @pl.when(jnp.logical_not(at_top))
        def _():
            passed(k, True).wait_recv()
            passed(k, False).wait_send()

        @pl.when(jnp.logical_not(at_bottom))
        def _():
            passed(k, False).wait_recv()
            passed(k, True).wait_send()

        return carry

    lax.fori_loop(0, n, settle, 0)
    for load in loads:
        load.wait()
    encoded = local_part(
        clips, me == 0, me == n - 1, at_top, at_bottom, clip_ref, recv, xs, w1, lt,
        wt, h1, h2, down, tdown, wout, tout, bin_ref, bdown_ref, bout_ref,
    )
    r, c = iota((256, 256), 0), iota((256, 256), 1)
    owner = jnp.zeros((256, 256), jnp.int32)
    for k in range(n):
        owner = owner + jnp.where(c % 16 == k, owner_ref[k], 0)
    spot = ((c // 16) % 2) * 8 + c // 32
    parts[...] = dot(one_hot(r, owner * 16 + spot), encoded).astype(BF).reshape(16, 16, 256)

    def part_to(k):
        to = lax.rem(me + k, n)
        return pltpu.make_async_remote_copy(
            src_ref=parts.at[to], dst_ref=landed.at[me], send_sem=send2_sem.at[k], recv_sem=recv2_sem.at[me],
            device_id={"tm": to}, device_id_type=MESH,
        )

    def part_from(k):
        source = lax.rem(me - k + n, n)
        return pltpu.make_async_remote_copy(
            src_ref=parts.at[me], dst_ref=landed.at[source], send_sem=send2_sem.at[k], recv_sem=recv2_sem.at[source],
            device_id={"tm": source}, device_id_type=MESH,
        )

    def start_part(k, carry):
        part_to(k).start()
        return carry

    lax.fori_loop(1, n, start_part, 0)
    own = pltpu.make_async_copy(parts.at[me], landed.at[me], own_sem)
    own.start()
    own.wait()

    def end(k, carry):
        sent(k).wait_send()
        part_to(k).wait_send()
        part_from(k).wait_recv()
        return carry

    lax.fori_loop(1, n, end, 0)
    perm = one_hot(((r // 4) % 16) * 16 + (r // 64) * 4 + r % 4, c)
    out_ref[...] = dot(perm, landed[...].reshape(256, 256)).astype(BF).reshape(2, 2, 64, 256)


def per_device(
    haar_video, clip_lengths, block_owner, spatial_in, temporal_in, bias_in, spatial_down, temporal_down, bias_down,
    spatial_out, temporal_out, bias_out,
):
    clips = clip_lengths.shape[0]
    vmem, smem, hbm = (
        pl.BlockSpec(memory_space=pltpu.VMEM),
        pl.BlockSpec(memory_space=pltpu.SMEM),
        pl.BlockSpec(memory_space=pl.ANY),
    )
    dma = pltpu.SemaphoreType.DMA
    return pl.pallas_call(
        functools.partial(kernel, clips),
        out_shape=jax.ShapeDtypeStruct((2, 2, 64, 256), BF),
        in_specs=[vmem, smem, smem, vmem, vmem, vmem, hbm, hbm, vmem, hbm, hbm, vmem],
        out_specs=vmem,
        scratch_shapes=[
            pltpu.VMEM((16, 6528), BF),
            pltpu.VMEM((3, 16, 16, PATCH), BF),
            pltpu.VMEM((12, 4, 16, PATCH), BF),
            pltpu.VMEM((5, 768, 384), BF),
            pltpu.VMEM((2, 13, 9, 2, 16, 256), BF),
            pltpu.VMEM((2, 256, 256), BF),
            pltpu.VMEM((2, 7, 9, 2, 2, 16, 128), BF),
            pltpu.VMEM((4, 6, 2, 16, 256), BF),
            pltpu.VMEM(spatial_down.shape, BF),
            pltpu.VMEM(temporal_down.shape, BF),
            pltpu.VMEM(spatial_out.shape, BF),
            pltpu.VMEM(temporal_out.shape, BF),
            pltpu.VMEM((16, 16, 256), BF),
            pltpu.VMEM((16, 16, 256), BF),
            dma((4,)),
            dma,
            dma((16,)),
            dma((16,)),
            dma((2, 16)),
            dma((2, 16)),
            dma((16,)),
            dma((16,)),
        ],
        compiler_params=pltpu.CompilerParams(
            collective_id=0, has_side_effects=True, vmem_limit_bytes=62 * 2**20
        ),
    )(
        haar_video, clip_lengths, block_owner, spatial_in, temporal_in, bias_in.reshape(1, 128), spatial_down,
        temporal_down, bias_down.reshape(1, 256), spatial_out, temporal_out, bias_out.reshape(1, 256),
    )


def solution(mesh):
    placed = (P("tm", "tile", None), P(), P(), P(), P(), P(), P(), P(), P(), P(), P(), P())
    return jax.shard_map(
        per_device,
        mesh=mesh,
        in_specs=placed,
        out_specs=P("tm", "tile", None, None),
        check_vma=False,
    )
```

```python
import functools

import jax
import jax.numpy as jnp
from jax import lax
from jax.experimental import pallas as pl
from jax.experimental.pallas import tpu as pltpu
from jax.sharding import PartitionSpec as P

MESH = pl.DeviceIdType.MESH
BF, F32 = jnp.bfloat16, jnp.float32

GROUPS = ((0, 0, 3), (1, 3, 3), (2, 6, 2), (3, 8, 3), (4, 11, 2))
PATCH = 768
STEP = 384


def iota(shape, dim):
    return lax.broadcasted_iota(jnp.int32, shape, dim)


def dot(a, b):
    return jnp.dot(a, b, preferred_element_type=F32)


def silu(v):
    return (0.5 * v) * (1.0 + jnp.tanh(0.5 * v))


def one_hot(row_key, col_key):
    return jnp.where(row_key == col_key, 1.0, 0.0).astype(BF)


def clip_masks(clip_ref, clips):
    base = 4 * iota((16, 128), 0)
    ends, end = [], 0
    for k in range(clips):
        end = end + clip_ref[k]
        ends.append(end)
    ids = {}
    for i in range(-3, 4):
        ids[i] = sum(jnp.where(base + i >= e, 1, 0) for e in ends)

    def same(key, tap):
        return jnp.where((ids[key] == ids[tap]) & (base + tap >= 0), 1.0, 0.0)

    return same


def build_first_weights(win_ref, w1_ref):
    for g, (window, first, count) in enumerate(GROUPS):
        w1_ref[g] = jnp.zeros(w1_ref.shape[1:], BF)
        for a in range(3):
            for b in range(3):
                for n in range(count):
                    at = a * 256 + 48 * (first + n + b) - 128 * window
                    w1_ref[g, at : at + 48, n * 128 : (n + 1) * 128] = win_ref[a, b]


def build_temporal_weights(tin_ref, wt_ref):
    zero = jnp.zeros((128, 128), BF)
    blocks = (((0, None), (None, 2)), ((1, 0), (2, 1)))
    for part in range(2):
        for i in range(2):
            for j in range(2):
                k = blocks[part][i][j]
                wt_ref[part, i * 128 : (i + 1) * 128, j * 128 : (j + 1) * 128] = (
                    zero if k is None else tin_ref[k]
                )


def spread(recv_ref, x_ref, rel):
    row, col = iota((256, 256), 0), iota((256, 256), 1)
    perm = one_hot((row % 16) * 16 + ((row // 16) % 4) * 4 + row // 64, col)
    for half in range(2):
        lanes = slice(half * 384, half * 384 + 384)
        block = recv_ref[rel, :, :, lanes].reshape(256, 384)
        x_ref[pl.ds(4 * rel, 4), :, :, lanes] = (
            dot(perm, block).astype(BF).reshape(4, 4, 16, 384)
        )


def first_spatial(x_ref, w1_ref, lt_ref, masks, row0, rows):
    left, right = slice(0, 128), slice(128, 256)
    for g, (window, first, count) in enumerate(GROUPS):
        lanes = slice(128 * window, 128 * window + 256)
        taps = [
            x_ref[pl.ds(row0 + a, rows), :, :, lanes].reshape(rows * 64, 256)
            for a in range(3)
        ]
        made = dot(jnp.concatenate(taps, axis=1), w1_ref[g, :, : count * 128])
        for n in range(count):
            s = made[:, n * 128 : (n + 1) * 128].reshape(rows, 4, 16, 128)
            late = s[:, 2:4].reshape(rows * 32, 128)
            late = pltpu.roll(late, 1, 0).reshape(rows, 2, 16, 128)

            def put(part, pair, lanes, value):
                lt_ref[part, first + n, pl.ds(row0, rows), pair, :, lanes] = value.astype(BF)

            put(0, 0, left, late[:, 0] * masks[0])
            put(0, 0, right, s[:, 1])
            put(1, 0, left, late[:, 1] * masks[1])
            put(1, 0, right, s[:, 0])
            put(0, 1, left, s[:, 0] * masks[2])
            put(0, 1, right, s[:, 3])
            put(1, 1, left, s[:, 1] * masks[3])
            put(1, 1, right, s[:, 2])


def first_temporal(lt_ref, wt_ref, h1_ref, bias, pair_mask, row0, rows):
    for col in range(13):
        one, two = (
            dot(lt_ref[i, col, pl.ds(row0, rows)].reshape(rows * 32, 256), wt_ref[i]).reshape(rows, 2, 16, 256)
            for i in range(2)
        )
        early = one[..., :128] + two[..., :128] + bias
        late = one[..., 128:] + two[..., 128:] * pair_mask[None] + bias
        h1_ref[col % 2, col // 2, pl.ds(row0, rows), :, 0] = silu(early).astype(BF)
        h1_ref[col % 2, col // 2, pl.ds(row0, rows), :, 1] = silu(late).astype(BF)


def second(h1_ref, down_ref, tdown_ref, h2_ref, bias, masks, q):
    taps = [
        h1_ref[b % 2, b // 2 : b // 2 + 6, 2 * q + a].reshape(384, 128)
        for a in range(3)
        for b in range(3)
    ]
    s = dot(jnp.concatenate(taps, axis=1), down_ref[...].reshape(1152, 256))
    s = s.reshape(6, 2, 2, 16, 256)
    before = pltpu.roll(s[:, 1, 1].reshape(96, 256), 1, 0).reshape(6, 1, 16, 256)
    k0 = jnp.concatenate([before, s[:, 0:1, 1]], axis=1) * masks[0]
    k1 = s[:, :, 0] * masks[1]
    k2 = s[:, :, 1]
    taps = jnp.concatenate([k.astype(BF).reshape(192, 256) for k in (k0, k1, k2)], axis=1)
    made = dot(taps, tdown_ref[...].reshape(768, 256)) + bias
    h2_ref[q] = silu(made).astype(BF).reshape(6, 2, 16, 256)


def third(h2_ref, wout_ref, tout_ref, bias, masks):
    taps = [
        h2_ref[a : a + 2, b : b + 4].reshape(256, 256) for a in range(3) for b in range(3)
    ]
    s = dot(jnp.concatenate(taps, axis=1), wout_ref[...].reshape(2304, 256))
    before = pltpu.roll(s, 1, 0).reshape(8, 2, 16, 256)
    s = s.reshape(8, 2, 16, 256)
    k0 = before * masks[0]
    k1 = jnp.concatenate([before[:, 1:2], s[:, 0:1]], axis=1) * masks[1]
    taps = jnp.concatenate([k.astype(BF).reshape(256, 256) for k in (k0, k1, s)], axis=1)
    return (dot(taps, tout_ref[...].reshape(768, 256)) + bias).astype(BF)


OFFSETS = sorted(
    ((dx, dy) for dx in range(4) for dy in range(4) if dx or dy),
    key=lambda o: (-min(o[0], 4 - o[0]) - min(o[1], 4 - o[1]), o),
)


def kernel(
    clips,
    x_hbm, clip_hbm, owner_hbm, win_hbm, tin_hbm, bin_hbm, down_hbm, tdown_hbm, bdown_hbm, wout_hbm, tout_hbm, bout_hbm,
    landed,
    x_in, clip_ref, owner_ref, win_ref, tin_ref, bin_ref, down, tdown, bdown_ref, wout, tout, bout_ref,
    xpad, recv, xs, w1, lt, wt, h1, h2, parts,
    load_sem, own_sem, send_sem, recv_sem, fsend_sem, frecv_sem, send2_sem, recv2_sem,
):
    me, row = lax.axis_index("tm"), lax.axis_index("tile")
    n, n_rows = lax.axis_size("tm"), lax.axis_size("tile")
    core = lax.rem(row, 2)
    at_top, at_bottom = row == 0, row == n_rows - 1
    barrier = pltpu.get_barrier_semaphore()

    def beside(dx, dy):
        return lax.rem(me // 4 + dx, 4) * 4 + lax.rem(lax.rem(me, 4) + dy, 4)

    for o in OFFSETS:
        pl.semaphore_signal(barrier, inc=1, device_id={"tm": beside(*o)}, device_id_type=MESH)

    @pl.when(jnp.logical_not(at_top))
    def _():
        pl.semaphore_signal(barrier, inc=1, device_id={"tile": row - 1}, device_id_type=MESH)

    @pl.when(jnp.logical_not(at_bottom))
    def _():
        pl.semaphore_signal(barrier, inc=1, device_id={"tile": row + 1}, device_id_type=MESH)

    x_load, *loads = [
        pltpu.make_async_copy(source, target, load_sem.at[i])
        for i, (source, target) in enumerate(
            (
                (x_hbm, x_in), (clip_hbm, clip_ref), (owner_hbm, owner_ref), (win_hbm, win_ref), (tin_hbm, tin_ref),
                (bin_hbm, bin_ref), (bdown_hbm, bdown_ref), (bout_hbm, bout_ref), (down_hbm, down),
                (tdown_hbm, tdown), (wout_hbm, wout), (tout_hbm, tout),
            )
        )
    ]
    x_load.start()
    for load in loads:
        load.start()
    x_load.wait()
    mine = jnp.concatenate([x_in[f].astype(F32) for f in range(4)], axis=0)
    side = jnp.zeros((16, 192), F32)
    xpad[...] = jnp.concatenate([side, mine, side], axis=1).astype(BF)
    pl.semaphore_wait(barrier, n - 1 + jnp.where(at_top, 0, 1) + jnp.where(at_bottom, 0, 1))

    def patch(who):
        return xpad.at[:, pl.ds(pl.multiple_of(who * STEP, 128), PATCH)]

    def across(i, o, source, target, send, recv_):
        to = beside(*o)
        return pltpu.make_async_remote_copy(
            src_ref=source(to), dst_ref=target(me), send_sem=send.at[i], recv_sem=recv_.at[me],
            device_id={"tm": to}, device_id_type=MESH,
        )

    def from_across(i, o, source, target, send, recv_):
        other = beside(-o[0] % 4, -o[1] % 4)
        return other, pltpu.make_async_remote_copy(
            src_ref=source(me), dst_ref=target(other), send_sem=send.at[i], recv_sem=recv_.at[other],
            device_id={"tm": other}, device_id_type=MESH,
        )

    out_way = (patch, lambda who: recv.at[1, who], send_sem, recv_sem)
    back_way = (lambda who: parts.at[who], lambda who: landed.at[who], send2_sem, recv2_sem)

    def passed(source, way):
        to = row + 1 - 2 * way
        return pltpu.make_async_remote_copy(
            src_ref=recv.at[1, source], dst_ref=recv.at[2 * way, source], send_sem=fsend_sem.at[way, source],
            recv_sem=frecv_sem.at[way, source], device_id={"tile": to}, device_id_type=MESH,
        )

    far_up, far_down = jnp.logical_and(core == 0, jnp.logical_not(at_top)), jnp.logical_and(core == 1, jnp.logical_not(at_bottom))

    def pass_on(source):
        @pl.when(jnp.logical_or(far_up, far_down))
        def _():
            passed(source, 1 - core).start()

        passed(source, core).start()

    for i, o in enumerate(OFFSETS):
        across(i, o, *out_way).start()
    own = pltpu.make_async_copy(patch(me), recv.at[1, me], own_sem)
    own.start()
    own.wait()
    pass_on(me)
    for load in loads[:7]:
        load.wait()
    build_first_weights(win_ref, w1)
    build_temporal_weights(tin_ref, wt)
    same = clip_masks(clip_ref, clips)
    bias_in, bias_down = bin_ref[...], bdown_ref[...]
    first_masks = [same(0, -2), same(0, -1), same(2, 0), same(2, 1)]
    pair_mask = jnp.stack([same(1, 0), same(3, 2)])

    def wide(one, two):
        both = jnp.stack([one, two])
        return jnp.concatenate([both, both], axis=2)

    second_masks = [wide(same(1, -1), same(3, 1)), wide(same(1, 0), same(3, 2))]
    third_masks = [wide(same(1, -3), same(3, -1)), wide(same(1, -1), same(3, 1))]

    @pl.when(at_top)
    def _():
        recv[0] = jnp.zeros(recv.shape[1:], BF)

    @pl.when(at_bottom)
    def _():
        recv[2] = jnp.zeros(recv.shape[1:], BF)

    for i, o in enumerate(OFFSETS):
        other, copy = from_across(i, o, *out_way)
        copy.wait_recv()
        pass_on(other)
    for load in loads[7:]:
        load.wait()
    spread(recv, xs, 1)

    def near(k, carry):
        passed(k, 1 - core).wait_recv()
        return carry

    lax.fori_loop(0, n, near, 0)
    spread(recv, xs, 2 * (1 - core))

    def section_one(row0, rows):
        first_spatial(xs, w1, lt, first_masks, row0, rows)
        first_temporal(lt, wt, h1, bias_in, pair_mask, row0, rows)

    def clear_left_one():
        @pl.when(me == 0)
        def _():
            h1[0, 1] = jnp.zeros((9, 2, 2, 16, 128), BF)

    section_one(4 * (1 - core), 5)
    clear_left_one()
    for q in range(2):
        second(h1, down, tdown, h2, bias_down, second_masks, 2 * (1 - core) + q)

    @pl.when(jnp.logical_or(far_up, far_down))
    def _():
        def far(k, carry):
            passed(k, core).wait_recv()
            return carry

        lax.fori_loop(0, n, far, 0)

    spread(recv, xs, 2 * core)
    section_one(5 * core, 4)
    clear_left_one()

    @pl.when(at_top)
    def _():
        h1[:, :, 2] = jnp.zeros((2, 7, 2, 2, 16, 128), BF)

    for q in range(2):
        second(h1, down, tdown, h2, bias_down, second_masks, 2 * core + q)

    @pl.when(at_top)
    def _():
        h2[0] = jnp.zeros((6, 2, 16, 256), BF)

    @pl.when(at_bottom)
    def _():
        h2[3] = jnp.zeros((6, 2, 16, 256), BF)

    @pl.when(me == 0)
    def _():
        h2[:, 0] = jnp.zeros((4, 2, 16, 256), BF)

    @pl.when(me == n - 1)
    def _():
        h2[:, 5] = jnp.zeros((4, 2, 16, 256), BF)

    encoded = third(h2, wout, tout, bout_ref[...], third_masks)
    r, c = iota((256, 256), 0), iota((256, 256), 1)
    owner = jnp.zeros((8, 256), jnp.int32)
    for k in range(n):
        owner = owner + jnp.where(iota((8, 256), 1) % 16 == k, owner_ref[k], 0)
    spot = ((c // 16) % 2) * 8 + c // 32
    parts[...] = dot(one_hot(r, owner[:1] * 16 + spot), encoded).astype(BF).reshape(16, 16, 256)
    for i, o in enumerate(OFFSETS):
        across(i, o, *back_way).start()
    own = pltpu.make_async_copy(parts.at[me], landed.at[me], own_sem)
    own.start()
    own.wait()
    for i, o in enumerate(OFFSETS):
        across(i, o, *out_way).wait_send()

    def settle(k, carry):
        passed(k, core).wait_send()
        return carry

    lax.fori_loop(0, n, settle, 0)

    @pl.when(jnp.logical_or(far_up, far_down))
    def _():
        def settle_far(k, carry):
            passed(k, 1 - core).wait_send()
            return carry

        lax.fori_loop(0, n, settle_far, 0)

    for i, o in enumerate(OFFSETS):
        across(i, o, *back_way).wait_send()
        from_across(i, o, *back_way)[1].wait_recv()


def lay_out(landed, out_ref):
    r, c = iota((256, 256), 0), iota((256, 256), 1)
    perm = one_hot(((r // 4) % 16) * 16 + (r // 64) * 4 + r % 4, c)
    out_ref[...] = dot(perm, landed[...].reshape(256, 256)).astype(BF).reshape(2, 2, 64, 256)


def per_device(
    haar_video, clip_lengths, block_owner, spatial_in, temporal_in, bias_in, spatial_down, temporal_down, bias_down,
    spatial_out, temporal_out, bias_out,
):
    clips = clip_lengths.shape[0]
    vmem, hbm = pl.BlockSpec(memory_space=pltpu.VMEM), pl.BlockSpec(memory_space=pl.ANY)
    dma = pltpu.SemaphoreType.DMA
    landed = pl.pallas_call(
        functools.partial(kernel, clips),
        out_shape=jax.ShapeDtypeStruct((16, 16, 256), BF),
        in_specs=[hbm] * 12,
        out_specs=vmem,
        scratch_shapes=[
            pltpu.VMEM(haar_video.shape, BF),
            pltpu.SMEM(clip_lengths.shape, jnp.int32),
            pltpu.SMEM(block_owner.shape, jnp.int32),
            pltpu.VMEM(spatial_in.shape, BF),
            pltpu.VMEM(temporal_in.shape, BF),
            pltpu.VMEM((1, 128), F32),
            pltpu.VMEM(spatial_down.shape, BF),
            pltpu.VMEM(temporal_down.shape, BF),
            pltpu.VMEM((1, 256), F32),
            pltpu.VMEM(spatial_out.shape, BF),
            pltpu.VMEM(temporal_out.shape, BF),
            pltpu.VMEM((1, 256), F32),
            pltpu.VMEM((16, 6528), BF),
            pltpu.VMEM((3, 16, 16, PATCH), BF),
            pltpu.VMEM((12, 4, 16, PATCH), BF),
            pltpu.VMEM((5, 768, 384), BF),
            pltpu.VMEM((2, 13, 9, 2, 16, 256), BF),
            pltpu.VMEM((2, 256, 256), BF),
            pltpu.VMEM((2, 7, 9, 2, 2, 16, 128), BF),
            pltpu.VMEM((4, 6, 2, 16, 256), BF),
            pltpu.VMEM((16, 16, 256), BF),
            dma((12,)),
            dma,
            dma((15,)),
            dma((16,)),
            dma((2, 16)),
            dma((2, 16)),
            dma((15,)),
            dma((16,)),
        ],
        compiler_params=pltpu.CompilerParams(
            collective_id=0, has_side_effects=True, vmem_limit_bytes=62 * 2**20
        ),
    )(
        haar_video, clip_lengths, block_owner, spatial_in, temporal_in, bias_in.reshape(1, 128), spatial_down,
        temporal_down, bias_down.reshape(1, 256), spatial_out, temporal_out, bias_out.reshape(1, 256),
    )
    return pl.pallas_call(
        lay_out,
        out_shape=jax.ShapeDtypeStruct((2, 2, 64, 256), BF),
        in_specs=[vmem],
        out_specs=vmem,
    )(landed)


def solution(mesh):
    placed = (P("tm", "tile", None), P(), P(), P(), P(), P(), P(), P(), P(), P(), P(), P())
    return jax.shard_map(
        per_device,
        mesh=mesh,
        in_specs=placed,
        out_specs=P("tm", "tile", None, None),
        check_vma=False,
    )
```

```python
import functools

import jax
import jax.numpy as jnp
from jax import lax
from jax.experimental import pallas as pl
from jax.experimental.pallas import tpu as pltpu
from jax.sharding import PartitionSpec as P

MESH = pl.DeviceIdType.MESH
BF, F32 = jnp.bfloat16, jnp.float32

GROUPS = ((0, 0, 3), (1, 3, 3), (2, 6, 2), (3, 8, 3), (4, 11, 2))
PATCH = 768
STEP = 384


def iota(shape, dim):
    return lax.broadcasted_iota(jnp.int32, shape, dim)


def dot(a, b):
    return jnp.dot(a, b, preferred_element_type=F32)


def silu(v):
    return (0.5 * v) * (1.0 + jnp.tanh(0.5 * v))


def one_hot(row_key, col_key):
    return jnp.where(row_key == col_key, 1.0, 0.0).astype(BF)


def clip_masks(clip_ref, clips):
    base = 4 * iota((16, 128), 0)
    ends, end = [], 0
    for k in range(clips):
        end = end + clip_ref[k]
        ends.append(end)
    ids = {}
    for i in range(-3, 4):
        ids[i] = sum(jnp.where(base + i >= e, 1, 0) for e in ends)

    def same(key, tap):
        return jnp.where((ids[key] == ids[tap]) & (base + tap >= 0), 1.0, 0.0)

    return same


def build_first_weights(win_ref, w1_ref):
    for g, (window, first, count) in enumerate(GROUPS):
        w1_ref[g] = jnp.zeros(w1_ref.shape[1:], BF)
        for a in range(3):
            for b in range(3):
                for n in range(count):
                    at = a * 256 + 48 * (first + n + b) - 128 * window
                    w1_ref[g, at : at + 48, n * 128 : (n + 1) * 128] = win_ref[a, b]


def build_temporal_weights(tin_ref, wt_ref):
    zero = jnp.zeros((128, 128), BF)
    blocks = (((0, None), (None, 2)), ((1, 0), (2, 1)))
    for part in range(2):
        for i in range(2):
            for j in range(2):
                k = blocks[part][i][j]
                wt_ref[part, i * 128 : (i + 1) * 128, j * 128 : (j + 1) * 128] = (
                    zero if k is None else tin_ref[k]
                )


def spread(recv_ref, perm_ref, x_ref, rel):
    for half in range(2):
        lanes = slice(half * 384, half * 384 + 384)
        block = recv_ref[rel, :, :, lanes].reshape(256, 384)
        x_ref[pl.ds(4 * rel, 4), :, :, lanes] = (
            dot(perm_ref[0], block).astype(BF).reshape(4, 4, 16, 384)
        )


def first_spatial(x_ref, w1_ref, lt_ref, masks, row0, rows):
    left, right = slice(0, 128), slice(128, 256)
    for g, (window, first, count) in enumerate(GROUPS):
        lanes = slice(128 * window, 128 * window + 256)
        taps = [
            x_ref[pl.ds(row0 + a, rows), :, :, lanes].reshape(rows * 64, 256)
            for a in range(3)
        ]
        made = dot(jnp.concatenate(taps, axis=1), w1_ref[g, :, : count * 128])
        for n in range(count):
            s = made[:, n * 128 : (n + 1) * 128].reshape(rows, 4, 16, 128)
            late = s[:, 2:4].reshape(rows * 32, 128)
            late = pltpu.roll(late, 1, 0).reshape(rows, 2, 16, 128)

            def put(part, pair, lanes, value):
                lt_ref[part, first + n, pl.ds(row0, rows), pair, :, lanes] = value.astype(BF)

            put(0, 0, left, late[:, 0] * masks[0])
            put(0, 0, right, s[:, 1])
            put(1, 0, left, late[:, 1] * masks[1])
            put(1, 0, right, s[:, 0])
            put(0, 1, left, s[:, 0] * masks[2])
            put(0, 1, right, s[:, 3])
            put(1, 1, left, s[:, 1] * masks[3])
            put(1, 1, right, s[:, 2])


def first_temporal(lt_ref, wt_ref, h1_ref, bias, pair_mask, row0, rows):
    for col in range(13):
        one, two = (
            dot(lt_ref[i, col, pl.ds(row0, rows)].reshape(rows * 32, 256), wt_ref[i]).reshape(rows, 2, 16, 256)
            for i in range(2)
        )
        early = one[..., :128] + two[..., :128] + bias
        late = one[..., 128:] + two[..., 128:] * pair_mask[None] + bias
        side = slice(col % 2 * 128, col % 2 * 128 + 128)
        h1_ref[col // 2, pl.ds(row0, rows), :, 0, :, side] = silu(early).astype(BF)
        h1_ref[col // 2, pl.ds(row0, rows), :, 1, :, side] = silu(late).astype(BF)


def build_down_weights(down_ref, wd_ref):
    for a in range(3):
        for b in range(2):
            wd_ref[256 * a + 128 * b : 256 * a + 128 * b + 128] = down_ref[a, b]
        wd_ref[768 + 128 * a : 896 + 128 * a] = down_ref[a, 2]


def second(h1_ref, wd_ref, tdown_ref, h2_ref, bias, masks, q):
    def tap(a, cols, lanes):
        two = [h1_ref[cols, 2 * q + 2 * i + a, :, :, :, lanes].reshape(384, -1) for i in range(2)]
        return jnp.concatenate(two, axis=0)

    taps = [tap(a, slice(0, 6), slice(0, 256)) for a in range(3)]
    taps += [tap(a, slice(1, 7), slice(0, 128)) for a in range(3)]
    s = dot(jnp.concatenate(taps, axis=1), wd_ref[...]).reshape(12, 2, 2, 16, 256)
    before = pltpu.roll(s[:, 1, 1].reshape(192, 256), 1, 0).reshape(12, 1, 16, 256)
    k0 = jnp.concatenate([before, s[:, 0:1, 1]], axis=1) * masks[0]
    k1 = s[:, :, 0] * masks[1]
    k2 = s[:, :, 1]
    taps = jnp.concatenate([k.astype(BF).reshape(384, 256) for k in (k0, k1, k2)], axis=1)
    made = dot(taps, tdown_ref[...].reshape(768, 256)) + bias
    h2_ref[pl.ds(q, 2)] = silu(made).astype(BF).reshape(2, 6, 2, 16, 256)


def third(h2_ref, wout_ref, tout_ref, bias, masks):
    taps = [
        h2_ref[a : a + 2, b : b + 4].reshape(256, 256) for a in range(3) for b in range(3)
    ]
    s = dot(jnp.concatenate(taps, axis=1), wout_ref[...].reshape(2304, 256))
    before = pltpu.roll(s, 1, 0).reshape(8, 2, 16, 256)
    s = s.reshape(8, 2, 16, 256)
    k0 = before * masks[0]
    k1 = jnp.concatenate([before[:, 1:2], s[:, 0:1]], axis=1) * masks[1]
    taps = jnp.concatenate([k.astype(BF).reshape(256, 256) for k in (k0, k1, s)], axis=1)
    return (dot(taps, tout_ref[...].reshape(768, 256)) + bias).astype(BF)


OFFSETS = sorted(
    ((dx, dy) for dx in range(4) for dy in range(4) if dx or dy),
    key=lambda o: (-min(o[0], 4 - o[0]) - min(o[1], 4 - o[1]), o),
)


def kernel(
    clips,
    x_hbm, clip_hbm, owner_hbm, win_hbm, tin_hbm, bin_hbm, down_hbm, tdown_hbm, bdown_hbm, wout_hbm, tout_hbm, bout_hbm,
    landed,
    x_in, clip_ref, owner_ref, win_ref, tin_ref, bin_ref, down, tdown, bdown_ref, wout, tout, bout_ref,
    xpad, recv, perms, xs, w1, wd, lt, wt, h1, h2, parts,
    load_sem, own_sem, send_sem, recv_sem, fsend_sem, frecv_sem, send2_sem, recv2_sem,
):
    me, row = lax.axis_index("tm"), lax.axis_index("tile")
    n, n_rows = lax.axis_size("tm"), lax.axis_size("tile")
    core = lax.rem(row, 2)
    at_top, at_bottom = row == 0, row == n_rows - 1
    barrier = pltpu.get_barrier_semaphore()

    def beside(dx, dy):
        return lax.rem(me // 4 + dx, 4) * 4 + lax.rem(lax.rem(me, 4) + dy, 4)

    for o in OFFSETS:
        pl.semaphore_signal(barrier, inc=1, device_id={"tm": beside(*o)}, device_id_type=MESH)

    @pl.when(jnp.logical_not(at_top))
    def _():
        pl.semaphore_signal(barrier, inc=1, device_id={"tile": row - 1}, device_id_type=MESH)

    @pl.when(jnp.logical_not(at_bottom))
    def _():
        pl.semaphore_signal(barrier, inc=1, device_id={"tile": row + 1}, device_id_type=MESH)

    x_load, *loads = [
        pltpu.make_async_copy(source, target, load_sem.at[i])
        for i, (source, target) in enumerate(
            (
                (x_hbm, x_in), (clip_hbm, clip_ref), (owner_hbm, owner_ref), (win_hbm, win_ref), (tin_hbm, tin_ref),
                (bin_hbm, bin_ref), (bdown_hbm, bdown_ref), (bout_hbm, bout_ref), (down_hbm, down),
                (tdown_hbm, tdown), (wout_hbm, wout), (tout_hbm, tout),
            )
        )
    ]
    x_load.start()
    for load in loads:
        load.start()
    x_load.wait()
    mine = jnp.concatenate([x_in[f].astype(F32) for f in range(4)], axis=0)
    side = jnp.zeros((16, 192), F32)
    xpad[...] = jnp.concatenate([side, mine, side], axis=1).astype(BF)
    pl.semaphore_wait(barrier, n - 1 + jnp.where(at_top, 0, 1) + jnp.where(at_bottom, 0, 1))

    def patch(who):
        return xpad.at[:, pl.ds(pl.multiple_of(who * STEP, 128), PATCH)]

    def across(i, o, source, target, send, recv_):
        to = beside(*o)
        return pltpu.make_async_remote_copy(
            src_ref=source(to), dst_ref=target(me), send_sem=send.at[i], recv_sem=recv_.at[me],
            device_id={"tm": to}, device_id_type=MESH,
        )

    def from_across(i, o, source, target, send, recv_):
        other = beside(-o[0] % 4, -o[1] % 4)
        return other, pltpu.make_async_remote_copy(
            src_ref=source(me), dst_ref=target(other), send_sem=send.at[i], recv_sem=recv_.at[other],
            device_id={"tm": other}, device_id_type=MESH,
        )

    out_way = (patch, lambda who: recv.at[1, who], send_sem, recv_sem)
    back_way = (lambda who: parts.at[who], lambda who: landed.at[who], send2_sem, recv2_sem)

    def passed(source, way):
        to = row + 1 - 2 * way
        return pltpu.make_async_remote_copy(
            src_ref=recv.at[1, source], dst_ref=recv.at[2 * way, source], send_sem=fsend_sem.at[way, source],
            recv_sem=frecv_sem.at[way, source], device_id={"tile": to}, device_id_type=MESH,
        )

    far_up, far_down = jnp.logical_and(core == 0, jnp.logical_not(at_top)), jnp.logical_and(core == 1, jnp.logical_not(at_bottom))

    def pass_on(source):
        @pl.when(jnp.logical_or(far_up, far_down))
        def _():
            passed(source, 1 - core).start()

        passed(source, core).start()

    for i, o in enumerate(OFFSETS):
        across(i, o, *out_way).start()
    own = pltpu.make_async_copy(patch(me), recv.at[1, me], own_sem)
    own.start()
    own.wait()
    pass_on(me)
    for load in loads:
        load.wait()
    build_first_weights(win_ref, w1)
    build_temporal_weights(tin_ref, wt)
    build_down_weights(down, wd)
    r, c = iota((256, 256), 0), iota((256, 256), 1)
    perms[0] = one_hot((r % 16) * 16 + ((r // 16) % 4) * 4 + r // 64, c)
    owner = jnp.zeros((8, 256), jnp.int32)
    for k in range(n):
        owner = owner + jnp.where(iota((8, 256), 1) % 16 == k, owner_ref[k], 0)
    spot = ((c // 16) % 2) * 8 + c // 32
    perms[1] = one_hot(r, owner[:1] * 16 + spot)
    same = clip_masks(clip_ref, clips)
    bias_in, bias_down = bin_ref[...], bdown_ref[...]
    first_masks = [same(0, -2), same(0, -1), same(2, 0), same(2, 1)]
    pair_mask = jnp.stack([same(1, 0), same(3, 2)])

    def wide(one, two):
        both = jnp.stack([one, two])
        return jnp.concatenate([both, both], axis=2)

    second_masks = [wide(same(1, -1), same(3, 1)), wide(same(1, 0), same(3, 2))]
    third_masks = [wide(same(1, -3), same(3, -1)), wide(same(1, -1), same(3, 1))]

    @pl.when(at_top)
    def _():
        recv[0] = jnp.zeros(recv.shape[1:], BF)

    @pl.when(at_bottom)
    def _():
        recv[2] = jnp.zeros(recv.shape[1:], BF)

    for i, o in enumerate(OFFSETS):
        other, copy = from_across(i, o, *out_way)
        copy.wait_recv()
        pass_on(other)
    spread(recv, perms, xs, 1)

    def near(k, carry):
        passed(k, 1 - core).wait_recv()
        return carry

    lax.fori_loop(0, n, near, 0)
    spread(recv, perms, xs, 2 * (1 - core))

    def section_one(row0, rows):
        first_spatial(xs, w1, lt, first_masks, row0, rows)
        first_temporal(lt, wt, h1, bias_in, pair_mask, row0, rows)

    def clear_left_one():
        @pl.when(me == 0)
        def _():
            h1[1, :, :, :, :, :128] = jnp.zeros((9, 2, 2, 16, 128), BF)

    section_one(4 * (1 - core), 5)
    clear_left_one()
    second(h1, wd, tdown, h2, bias_down, second_masks, 2 * (1 - core))

    @pl.when(jnp.logical_or(far_up, far_down))
    def _():
        def far(k, carry):
            passed(k, core).wait_recv()
            return carry

        lax.fori_loop(0, n, far, 0)

    spread(recv, perms, xs, 2 * core)
    section_one(5 * core, 4)
    clear_left_one()

    @pl.when(at_top)
    def _():
        h1[:, 2] = jnp.zeros((7, 2, 2, 16, 256), BF)

    second(h1, wd, tdown, h2, bias_down, second_masks, 2 * core)

    @pl.when(at_top)
    def _():
        h2[0] = jnp.zeros((6, 2, 16, 256), BF)

    @pl.when(at_bottom)
    def _():
        h2[3] = jnp.zeros((6, 2, 16, 256), BF)

    @pl.when(me == 0)
    def _():
        h2[:, 0] = jnp.zeros((4, 2, 16, 256), BF)

    @pl.when(me == n - 1)
    def _():
        h2[:, 5] = jnp.zeros((4, 2, 16, 256), BF)

    encoded = third(h2, wout, tout, bout_ref[...], third_masks)
    parts[...] = dot(perms[1], encoded).astype(BF).reshape(16, 16, 256)
    for i, o in enumerate(OFFSETS):
        across(i, o, *back_way).start()
    own = pltpu.make_async_copy(parts.at[me], landed.at[me], own_sem)
    own.start()
    own.wait()
    for i, o in enumerate(OFFSETS):
        across(i, o, *out_way).wait_send()

    def settle(k, carry):
        passed(k, core).wait_send()
        return carry

    lax.fori_loop(0, n, settle, 0)

    @pl.when(jnp.logical_or(far_up, far_down))
    def _():
        def settle_far(k, carry):
            passed(k, 1 - core).wait_send()
            return carry

        lax.fori_loop(0, n, settle_far, 0)

    for i, o in enumerate(OFFSETS):
        across(i, o, *back_way).wait_send()
        from_across(i, o, *back_way)[1].wait_recv()


def lay_out(landed, out_ref):
    r, c = iota((256, 256), 0), iota((256, 256), 1)
    perm = one_hot(((r // 4) % 16) * 16 + (r // 64) * 4 + r % 4, c)
    out_ref[...] = dot(perm, landed[...].reshape(256, 256)).astype(BF).reshape(2, 2, 64, 256)


def per_device(
    haar_video, clip_lengths, block_owner, spatial_in, temporal_in, bias_in, spatial_down, temporal_down, bias_down,
    spatial_out, temporal_out, bias_out,
):
    clips = clip_lengths.shape[0]
    vmem, hbm = pl.BlockSpec(memory_space=pltpu.VMEM), pl.BlockSpec(memory_space=pl.ANY)
    dma = pltpu.SemaphoreType.DMA
    landed = pl.pallas_call(
        functools.partial(kernel, clips),
        out_shape=jax.ShapeDtypeStruct((16, 16, 256), BF),
        in_specs=[hbm] * 12,
        out_specs=hbm,
        scratch_shapes=[
            pltpu.VMEM(haar_video.shape, BF),
            pltpu.SMEM(clip_lengths.shape, jnp.int32),
            pltpu.SMEM(block_owner.shape, jnp.int32),
            pltpu.VMEM(spatial_in.shape, BF),
            pltpu.VMEM(temporal_in.shape, BF),
            pltpu.VMEM((1, 128), F32),
            pltpu.VMEM(spatial_down.shape, BF),
            pltpu.VMEM(temporal_down.shape, BF),
            pltpu.VMEM((1, 256), F32),
            pltpu.VMEM(spatial_out.shape, BF),
            pltpu.VMEM(temporal_out.shape, BF),
            pltpu.VMEM((1, 256), F32),
            pltpu.VMEM((16, 6528), BF),
            pltpu.VMEM((3, 16, 16, PATCH), BF),
            pltpu.VMEM((2, 256, 256), BF),
            pltpu.VMEM((12, 4, 16, PATCH), BF),
            pltpu.VMEM((5, 768, 384), BF),
            pltpu.VMEM((1152, 256), BF),
            pltpu.VMEM((2, 13, 9, 2, 16, 256), BF),
            pltpu.VMEM((2, 256, 256), BF),
            pltpu.VMEM((7, 9, 2, 2, 16, 256), BF),
            pltpu.VMEM((4, 6, 2, 16, 256), BF),
            pltpu.VMEM((16, 16, 256), BF),
            dma((12,)),
            dma,
            dma((15,)),
            dma((16,)),
            dma((2, 16)),
            dma((2, 16)),
            dma((15,)),
            dma((16,)),
        ],
        compiler_params=pltpu.CompilerParams(
            collective_id=0, has_side_effects=True, vmem_limit_bytes=62 * 2**20
        ),
    )(
        haar_video, clip_lengths, block_owner, spatial_in, temporal_in, bias_in.reshape(1, 128), spatial_down,
        temporal_down, bias_down.reshape(1, 256), spatial_out, temporal_out, bias_out.reshape(1, 256),
    )
    return pl.pallas_call(
        lay_out,
        out_shape=jax.ShapeDtypeStruct((2, 2, 64, 256), BF),
        in_specs=[vmem],
        out_specs=vmem,
    )(landed)


def solution(mesh):
    placed = (P("tm", "tile", None), P(), P(), P(), P(), P(), P(), P(), P(), P(), P(), P())
    return jax.shard_map(
        per_device,
        mesh=mesh,
        in_specs=placed,
        out_specs=P("tm", "tile", None, None),
        check_vma=False,
    )
```

```python
import functools

import jax
import jax.numpy as jnp
from jax import lax
from jax.experimental import pallas as pl
from jax.experimental.pallas import tpu as pltpu
from jax.sharding import PartitionSpec as P

MESH = pl.DeviceIdType.MESH
BF, F32 = jnp.bfloat16, jnp.float32

GROUPS = ((0, 0, 3), (1, 3, 3), (2, 6, 2), (3, 8, 3), (4, 11, 2))
PATCH = 768
STEP = 384


def iota(shape, dim):
    return lax.broadcasted_iota(jnp.int32, shape, dim)


def dot(a, b):
    return jnp.dot(a, b, preferred_element_type=F32)


def silu(v):
    return (0.5 * v) * (1.0 + jnp.tanh(0.5 * v))


def one_hot(row_key, col_key):
    return jnp.where(row_key == col_key, 1.0, 0.0).astype(BF)


def clip_masks(clip_ref, clips):
    base = 4 * iota((16, 128), 0)
    ends, end = [], 0
    for k in range(clips):
        end = end + clip_ref[k]
        ends.append(end)
    ids = {}
    for i in range(-3, 4):
        ids[i] = sum(jnp.where(base + i >= e, 1, 0) for e in ends)

    def same(key, tap):
        return jnp.where((ids[key] == ids[tap]) & (base + tap >= 0), 1.0, 0.0)

    return same


def build_first_weights(win_ref, w1_ref):
    for g, (window, first, count) in enumerate(GROUPS):
        w1_ref[g] = jnp.zeros(w1_ref.shape[1:], BF)
        for a in range(3):
            for b in range(3):
                for n in range(count):
                    at = a * 256 + 48 * (first + n + b) - 128 * window
                    w1_ref[g, at : at + 48, n * 128 : (n + 1) * 128] = win_ref[a, b]


def build_temporal_weights(tin_ref, wt_ref):
    zero = jnp.zeros((128, 128), BF)
    blocks = (((0, None), (None, 2)), ((1, 0), (2, 1)))
    for part in range(2):
        for i in range(2):
            for j in range(2):
                k = blocks[part][i][j]
                wt_ref[part, i * 128 : (i + 1) * 128, j * 128 : (j + 1) * 128] = (
                    zero if k is None else tin_ref[k]
                )


def spread(recv_ref, perm_ref, x_ref, rel):
    for half in range(2):
        lanes = slice(half * 384, half * 384 + 384)
        block = recv_ref[rel, :, :, lanes].reshape(256, 384)
        x_ref[pl.ds(4 * rel, 4), :, :, lanes] = (
            dot(perm_ref[0], block).astype(BF).reshape(4, 4, 16, 384)
        )


def first_spatial(x_ref, w1_ref, lt_ref, masks, row0, rows):
    left, right = slice(0, 128), slice(128, 256)
    for g, (window, first, count) in enumerate(GROUPS):
        lanes = slice(128 * window, 128 * window + 256)
        taps = [
            x_ref[pl.ds(row0 + a, rows), :, :, lanes].reshape(rows * 64, 256)
            for a in range(3)
        ]
        made = dot(jnp.concatenate(taps, axis=1), w1_ref[g, :, : count * 128])
        for n in range(count):
            s = made[:, n * 128 : (n + 1) * 128].reshape(rows, 4, 16, 128)
            late = s[:, 2:4].reshape(rows * 32, 128)
            late = pltpu.roll(late, 1, 0).reshape(rows, 2, 16, 128)

            def put(part, pair, lanes, value):
                lt_ref[part, first + n, pl.ds(row0, rows), pair, :, lanes] = value.astype(BF)

            put(0, 0, left, late[:, 0] * masks[0])
            put(0, 0, right, s[:, 1])
            put(1, 0, left, late[:, 1] * masks[1])
            put(1, 0, right, s[:, 0])
            put(0, 1, left, s[:, 0] * masks[2])
            put(0, 1, right, s[:, 3])
            put(1, 1, left, s[:, 1] * masks[3])
            put(1, 1, right, s[:, 2])


def first_temporal(lt_ref, wt_ref, h1_ref, bias, pair_mask, row0, rows):
    for col in range(13):
        one, two = (
            dot(lt_ref[i, col, pl.ds(row0, rows)].reshape(rows * 32, 256), wt_ref[i]).reshape(rows, 2, 16, 256)
            for i in range(2)
        )
        early = one[..., :128] + two[..., :128] + bias
        late = one[..., 128:] + two[..., 128:] * pair_mask[None] + bias
        side = slice(col % 2 * 128, col % 2 * 128 + 128)
        h1_ref[col // 2, pl.ds(row0, rows), :, 0, :, side] = silu(early).astype(BF)
        h1_ref[col // 2, pl.ds(row0, rows), :, 1, :, side] = silu(late).astype(BF)


def build_down_weights(down_ref, wd_ref):
    for a in range(3):
        for b in range(2):
            wd_ref[256 * a + 128 * b : 256 * a + 128 * b + 128] = down_ref[a, b]
        wd_ref[768 + 128 * a : 896 + 128 * a] = down_ref[a, 2]


def second(h1_ref, wd_ref, tdown_ref, h2_ref, bias, masks, q):
    def spatial(i):
        taps = [h1_ref[0:6, 2 * q + 2 * i + a].reshape(384, 256) for a in range(3)]
        taps += [h1_ref[1:7, 2 * q + 2 * i + a, :, :, :, :128].reshape(384, 128) for a in range(3)]
        return dot(jnp.concatenate(taps, axis=1), wd_ref[...]).reshape(6, 2, 2, 16, 256)

    def temporal(s):
        before = pltpu.roll(s[:, 1, 1].reshape(96, 256), 1, 0).reshape(6, 1, 16, 256)
        k0 = jnp.concatenate([before, s[:, 0:1, 1]], axis=1) * masks[0]
        k1 = s[:, :, 0] * masks[1]
        k2 = s[:, :, 1]
        taps = jnp.concatenate([k.astype(BF).reshape(192, 256) for k in (k0, k1, k2)], axis=1)
        return dot(taps, tdown_ref[...].reshape(768, 256)) + bias

    spread_out = [spatial(i) for i in range(2)]
    made = [temporal(s) for s in spread_out]
    for i in range(2):
        h2_ref[q + i] = silu(made[i]).astype(BF).reshape(6, 2, 16, 256)


def third(h2_ref, wout_ref, tout_ref, bias, masks):
    def spatial(q):
        taps = [h2_ref[q + a, b : b + 4].reshape(128, 256) for a in range(3) for b in range(3)]
        return dot(jnp.concatenate(taps, axis=1), wout_ref[...].reshape(2304, 256))

    def temporal(s):
        before = pltpu.roll(s, 1, 0).reshape(4, 2, 16, 256)
        s = s.reshape(4, 2, 16, 256)
        k0 = before * masks[0]
        k1 = jnp.concatenate([before[:, 1:2], s[:, 0:1]], axis=1) * masks[1]
        taps = jnp.concatenate([k.astype(BF).reshape(128, 256) for k in (k0, k1, s)], axis=1)
        return dot(taps, tout_ref[...].reshape(768, 256)) + bias

    made = [temporal(s) for s in [spatial(q) for q in range(2)]]
    return jnp.concatenate(made, axis=0).astype(BF)


OFFSETS = sorted(
    ((dx, dy) for dx in range(4) for dy in range(4) if dx or dy),
    key=lambda o: (-min(o[0], 4 - o[0]) - min(o[1], 4 - o[1]), o),
)


def kernel(
    clips,
    x_hbm, clip_hbm, owner_hbm, win_hbm, tin_hbm, bin_hbm, down_hbm, tdown_hbm, bdown_hbm, wout_hbm, tout_hbm, bout_hbm,
    landed,
    x_in, clip_ref, owner_ref, win_ref, tin_ref, bin_ref, down, tdown, bdown_ref, wout, tout, bout_ref,
    xpad, recv, perms, xs, w1, wd, lt, wt, h1, h2, parts,
    load_sem, own_sem, send_sem, recv_sem, fsend_sem, frecv_sem, send2_sem, recv2_sem,
):
    me, row = lax.axis_index("tm"), lax.axis_index("tile")
    n, n_rows = lax.axis_size("tm"), lax.axis_size("tile")
    core = lax.rem(row, 2)
    at_top, at_bottom = row == 0, row == n_rows - 1
    barrier = pltpu.get_barrier_semaphore()

    def beside(dx, dy):
        return lax.rem(me // 4 + dx, 4) * 4 + lax.rem(lax.rem(me, 4) + dy, 4)

    for o in OFFSETS:
        pl.semaphore_signal(barrier, inc=1, device_id={"tm": beside(*o)}, device_id_type=MESH)

    @pl.when(jnp.logical_not(at_top))
    def _():
        pl.semaphore_signal(barrier, inc=1, device_id={"tile": row - 1}, device_id_type=MESH)

    @pl.when(jnp.logical_not(at_bottom))
    def _():
        pl.semaphore_signal(barrier, inc=1, device_id={"tile": row + 1}, device_id_type=MESH)

    x_load, *loads = [
        pltpu.make_async_copy(source, target, load_sem.at[i])
        for i, (source, target) in enumerate(
            (
                (x_hbm, x_in), (clip_hbm, clip_ref), (owner_hbm, owner_ref), (win_hbm, win_ref), (tin_hbm, tin_ref),
                (bin_hbm, bin_ref), (bdown_hbm, bdown_ref), (bout_hbm, bout_ref), (down_hbm, down),
                (tdown_hbm, tdown), (wout_hbm, wout), (tout_hbm, tout),
            )
        )
    ]
    x_load.start()
    for load in loads:
        load.start()
    x_load.wait()
    mine = jnp.concatenate([x_in[f].astype(F32) for f in range(4)], axis=0)
    side = jnp.zeros((16, 192), F32)
    xpad[...] = jnp.concatenate([side, mine, side], axis=1).astype(BF)
    pl.semaphore_wait(barrier, n - 1 + jnp.where(at_top, 0, 1) + jnp.where(at_bottom, 0, 1))

    def patch(who):
        return xpad.at[:, pl.ds(pl.multiple_of(who * STEP, 128), PATCH)]

    def across(i, o, source, target, send, recv_):
        to = beside(*o)
        return pltpu.make_async_remote_copy(
            src_ref=source(to), dst_ref=target(me), send_sem=send.at[i], recv_sem=recv_.at[me],
            device_id={"tm": to}, device_id_type=MESH,
        )

    def from_across(i, o, source, target, send, recv_):
        other = beside(-o[0] % 4, -o[1] % 4)
        return other, pltpu.make_async_remote_copy(
            src_ref=source(me), dst_ref=target(other), send_sem=send.at[i], recv_sem=recv_.at[other],
            device_id={"tm": other}, device_id_type=MESH,
        )

    out_way = (patch, lambda who: recv.at[1, who], send_sem, recv_sem)
    back_way = (lambda who: parts.at[who], lambda who: landed.at[who], send2_sem, recv2_sem)

    def passed(source, way):
        to = row + 1 - 2 * way
        return pltpu.make_async_remote_copy(
            src_ref=recv.at[1, source], dst_ref=recv.at[2 * way, source], send_sem=fsend_sem.at[way, source],
            recv_sem=frecv_sem.at[way, source], device_id={"tile": to}, device_id_type=MESH,
        )

    far_up, far_down = jnp.logical_and(core == 0, jnp.logical_not(at_top)), jnp.logical_and(core == 1, jnp.logical_not(at_bottom))

    def pass_on(source):
        @pl.when(jnp.logical_or(far_up, far_down))
        def _():
            passed(source, 1 - core).start()

        passed(source, core).start()

    for i, o in enumerate(OFFSETS):
        across(i, o, *out_way).start()
    own = pltpu.make_async_copy(patch(me), recv.at[1, me], own_sem)
    own.start()
    own.wait()
    pass_on(me)
    for load in loads:
        load.wait()
    build_first_weights(win_ref, w1)
    build_temporal_weights(tin_ref, wt)
    build_down_weights(down, wd)
    r, c = iota((256, 256), 0), iota((256, 256), 1)
    perms[0] = one_hot((r % 16) * 16 + ((r // 16) % 4) * 4 + r // 64, c)
    owner = jnp.zeros((8, 256), jnp.int32)
    for k in range(n):
        owner = owner + jnp.where(iota((8, 256), 1) % 16 == k, owner_ref[k], 0)
    spot = ((c // 16) % 2) * 8 + c // 32
    perms[1] = one_hot(r, owner[:1] * 16 + spot)
    same = clip_masks(clip_ref, clips)
    bias_in, bias_down = bin_ref[...], bdown_ref[...]
    first_masks = [same(0, -2), same(0, -1), same(2, 0), same(2, 1)]
    pair_mask = jnp.stack([same(1, 0), same(3, 2)])

    def wide(one, two):
        both = jnp.stack([one, two])
        return jnp.concatenate([both, both], axis=2)

    second_masks = [wide(same(1, -1), same(3, 1)), wide(same(1, 0), same(3, 2))]
    third_masks = [wide(same(1, -3), same(3, -1)), wide(same(1, -1), same(3, 1))]

    @pl.when(at_top)
    def _():
        recv[0] = jnp.zeros(recv.shape[1:], BF)

    @pl.when(at_bottom)
    def _():
        recv[2] = jnp.zeros(recv.shape[1:], BF)

    for i, o in enumerate(OFFSETS):
        other, copy = from_across(i, o, *out_way)
        copy.wait_recv()
        pass_on(other)
    spread(recv, perms, xs, 1)

    def near(k, carry):
        passed(k, 1 - core).wait_recv()
        return carry

    lax.fori_loop(0, n, near, 0)
    spread(recv, perms, xs, 2 * (1 - core))

    def section_one(row0, rows):
        first_spatial(xs, w1, lt, first_masks, row0, rows)
        first_temporal(lt, wt, h1, bias_in, pair_mask, row0, rows)

    def clear_left_one():
        @pl.when(me == 0)
        def _():
            h1[1, :, :, :, :, :128] = jnp.zeros((9, 2, 2, 16, 128), BF)

    section_one(4 * (1 - core), 5)
    clear_left_one()
    second(h1, wd, tdown, h2, bias_down, second_masks, 2 * (1 - core))

    @pl.when(jnp.logical_or(far_up, far_down))
    def _():
        def far(k, carry):
            passed(k, core).wait_recv()
            return carry

        lax.fori_loop(0, n, far, 0)

    spread(recv, perms, xs, 2 * core)
    section_one(5 * core, 4)
    clear_left_one()

    @pl.when(at_top)
    def _():
        h1[:, 2] = jnp.zeros((7, 2, 2, 16, 256), BF)

    second(h1, wd, tdown, h2, bias_down, second_masks, 2 * core)

    @pl.when(at_top)
    def _():
        h2[0] = jnp.zeros((6, 2, 16, 256), BF)

    @pl.when(at_bottom)
    def _():
        h2[3] = jnp.zeros((6, 2, 16, 256), BF)

    @pl.when(me == 0)
    def _():
        h2[:, 0] = jnp.zeros((4, 2, 16, 256), BF)

    @pl.when(me == n - 1)
    def _():
        h2[:, 5] = jnp.zeros((4, 2, 16, 256), BF)

    encoded = third(h2, wout, tout, bout_ref[...], third_masks)
    parts[...] = dot(perms[1], encoded).astype(BF).reshape(16, 16, 256)
    for i, o in enumerate(OFFSETS):
        across(i, o, *back_way).start()
    own = pltpu.make_async_copy(parts.at[me], landed.at[me], own_sem)
    own.start()
    own.wait()
    for i, o in enumerate(OFFSETS):
        across(i, o, *out_way).wait_send()

    def settle(k, carry):
        passed(k, core).wait_send()
        return carry

    lax.fori_loop(0, n, settle, 0)

    @pl.when(jnp.logical_or(far_up, far_down))
    def _():
        def settle_far(k, carry):
            passed(k, 1 - core).wait_send()
            return carry

        lax.fori_loop(0, n, settle_far, 0)

    for i, o in enumerate(OFFSETS):
        across(i, o, *back_way).wait_send()
        from_across(i, o, *back_way)[1].wait_recv()


def lay_out(landed, out_ref):
    r, c = iota((256, 256), 0), iota((256, 256), 1)
    perm = one_hot(((r // 4) % 16) * 16 + (r // 64) * 4 + r % 4, c)
    out_ref[...] = dot(perm, landed[...].reshape(256, 256)).astype(BF).reshape(2, 2, 64, 256)


def per_device(
    haar_video, clip_lengths, block_owner, spatial_in, temporal_in, bias_in, spatial_down, temporal_down, bias_down,
    spatial_out, temporal_out, bias_out,
):
    clips = clip_lengths.shape[0]
    vmem, hbm = pl.BlockSpec(memory_space=pltpu.VMEM), pl.BlockSpec(memory_space=pl.ANY)
    dma = pltpu.SemaphoreType.DMA
    landed = pl.pallas_call(
        functools.partial(kernel, clips),
        out_shape=jax.ShapeDtypeStruct((16, 16, 256), BF),
        in_specs=[hbm] * 12,
        out_specs=hbm,
        scratch_shapes=[
            pltpu.VMEM(haar_video.shape, BF),
            pltpu.SMEM(clip_lengths.shape, jnp.int32),
            pltpu.SMEM(block_owner.shape, jnp.int32),
            pltpu.VMEM(spatial_in.shape, BF),
            pltpu.VMEM(temporal_in.shape, BF),
            pltpu.VMEM((1, 128), F32),
            pltpu.VMEM(spatial_down.shape, BF),
            pltpu.VMEM(temporal_down.shape, BF),
            pltpu.VMEM((1, 256), F32),
            pltpu.VMEM(spatial_out.shape, BF),
            pltpu.VMEM(temporal_out.shape, BF),
            pltpu.VMEM((1, 256), F32),
            pltpu.VMEM((16, 6528), BF),
            pltpu.VMEM((3, 16, 16, PATCH), BF),
            pltpu.VMEM((2, 256, 256), BF),
            pltpu.VMEM((12, 4, 16, PATCH), BF),
            pltpu.VMEM((5, 768, 384), BF),
            pltpu.VMEM((1152, 256), BF),
            pltpu.VMEM((2, 13, 9, 2, 16, 256), BF),
            pltpu.VMEM((2, 256, 256), BF),
            pltpu.VMEM((7, 9, 2, 2, 16, 256), BF),
            pltpu.VMEM((4, 6, 2, 16, 256), BF),
            pltpu.VMEM((16, 16, 256), BF),
            dma((12,)),
            dma,
            dma((15,)),
            dma((16,)),
            dma((2, 16)),
            dma((2, 16)),
            dma((15,)),
            dma((16,)),
        ],
        compiler_params=pltpu.CompilerParams(
            collective_id=0, has_side_effects=True, vmem_limit_bytes=62 * 2**20
        ),
    )(
        haar_video, clip_lengths, block_owner, spatial_in, temporal_in, bias_in.reshape(1, 128), spatial_down,
        temporal_down, bias_down.reshape(1, 256), spatial_out, temporal_out, bias_out.reshape(1, 256),
    )
    return pl.pallas_call(
        lay_out,
        out_shape=jax.ShapeDtypeStruct((2, 2, 64, 256), BF),
        in_specs=[vmem],
        out_specs=vmem,
    )(landed)


def solution(mesh):
    placed = (P("tm", "tile", None), P(), P(), P(), P(), P(), P(), P(), P(), P(), P(), P())
    return jax.shard_map(
        per_device,
        mesh=mesh,
        in_specs=placed,
        out_specs=P("tm", "tile", None, None),
        check_vma=False,
    )
```

```python
import functools

import jax
import jax.numpy as jnp
from jax import lax
from jax.experimental import pallas as pl
from jax.experimental.pallas import tpu as pltpu
from jax.sharding import PartitionSpec as P

MESH = pl.DeviceIdType.MESH
BF, F32 = jnp.bfloat16, jnp.float32

GROUPS = ((0, 0, 3), (1, 3, 3), (2, 6, 2), (3, 8, 3), (4, 11, 2))
PATCH = 768
STEP = 384


def iota(shape, dim):
    return lax.broadcasted_iota(jnp.int32, shape, dim)


def dot(a, b):
    return jnp.dot(a, b, preferred_element_type=F32)


def silu(v):
    return (0.5 * v) * (1.0 + jnp.tanh(0.5 * v))


def one_hot(row_key, col_key):
    return jnp.where(row_key == col_key, 1.0, 0.0).astype(BF)


def clip_masks(clip_ref, clips):
    base = 4 * iota((16, 128), 0)
    ends, end = [], 0
    for k in range(clips):
        end = end + clip_ref[k]
        ends.append(end)
    ids = {}
    for i in range(-3, 4):
        ids[i] = sum(jnp.where(base + i >= e, 1, 0) for e in ends)

    def same(key, tap):
        return jnp.where((ids[key] == ids[tap]) & (base + tap >= 0), 1.0, 0.0)

    return same


def build_first_weights(win_ref, w1_ref):
    for g, (window, first, count) in enumerate(GROUPS):
        for a in range(3):
            for b in range(3):
                for n in range(count):
                    at = a * 256 + 48 * (first + n + b) - 128 * window
                    w1_ref[g, at : at + 48, n * 128 : (n + 1) * 128] = win_ref[a, b]


def build_temporal_weights(tin_ref, wt_ref):
    zero = jnp.zeros((128, 128), BF)
    blocks = (((0, None), (None, 2)), ((1, 0), (2, 1)))
    for part in range(2):
        for i in range(2):
            for j in range(2):
                k = blocks[part][i][j]
                wt_ref[part, i * 128 : (i + 1) * 128, j * 128 : (j + 1) * 128] = (
                    zero if k is None else tin_ref[k]
                )


def spread(recv_ref, perm_ref, x_ref, rel):
    for half in range(2):
        lanes = slice(half * 384, half * 384 + 384)
        block = recv_ref[rel, :, :, lanes].reshape(256, 384)
        x_ref[pl.ds(4 * rel, 4), :, :, lanes] = (
            dot(perm_ref[0], block).astype(BF).reshape(4, 4, 16, 384)
        )


def first_spatial(x_ref, w1_ref, lt_ref, masks, row0, rows):
    left, right = slice(0, 128), slice(128, 256)
    for g, (window, first, count) in enumerate(GROUPS):
        lanes = slice(128 * window, 128 * window + 256)
        taps = [
            x_ref[pl.ds(row0 + a, rows), :, :, lanes].reshape(rows * 64, 256)
            for a in range(3)
        ]
        made = dot(jnp.concatenate(taps, axis=1), w1_ref[g, :, : count * 128])
        for n in range(count):
            s = made[:, n * 128 : (n + 1) * 128].reshape(rows, 4, 16, 128)
            late = s[:, 2:4].reshape(rows * 32, 128)
            late = pltpu.roll(late, 1, 0).reshape(rows, 2, 16, 128)

            def put(part, pair, lanes, value):
                lt_ref[part, first + n, pl.ds(row0, rows), pair, :, lanes] = value.astype(BF)

            put(0, 0, left, late[:, 0] * masks[0])
            put(0, 0, right, s[:, 1])
            put(1, 0, left, late[:, 1] * masks[1])
            put(1, 0, right, s[:, 0])
            put(0, 1, left, s[:, 0] * masks[2])
            put(0, 1, right, s[:, 3])
            put(1, 1, left, s[:, 1] * masks[3])
            put(1, 1, right, s[:, 2])


def first_temporal(lt_ref, wt_ref, h1_ref, bias, pair_mask, row0, rows):
    for col in range(13):
        one, two = (
            dot(lt_ref[i, col, pl.ds(row0, rows)].reshape(rows * 32, 256), wt_ref[i]).reshape(rows, 2, 16, 256)
            for i in range(2)
        )
        early = one[..., :128] + two[..., :128] + bias
        late = one[..., 128:] + two[..., 128:] * pair_mask[None] + bias
        side = slice(col % 2 * 128, col % 2 * 128 + 128)
        h1_ref[col // 2, pl.ds(row0, rows), :, 0, :, side] = silu(early).astype(BF)
        h1_ref[col // 2, pl.ds(row0, rows), :, 1, :, side] = silu(late).astype(BF)


def second(h1_ref, down_ref, tdown_ref, h2_ref, bias, masks, q):
    def spatial(i):
        taps = []
        for a in range(3):
            taps.append(h1_ref[0:6, 2 * q + 2 * i + a].reshape(384, 256))
            taps.append(h1_ref[1:7, 2 * q + 2 * i + a, :, :, :, :128].reshape(384, 128))
        return dot(jnp.concatenate(taps, axis=1), down_ref[...].reshape(1152, 256)).reshape(6, 2, 2, 16, 256)

    def temporal(s):
        before = pltpu.roll(s[:, 1, 1].reshape(96, 256), 1, 0).reshape(6, 1, 16, 256)
        k0 = jnp.concatenate([before, s[:, 0:1, 1]], axis=1) * masks[0]
        k1 = s[:, :, 0] * masks[1]
        k2 = s[:, :, 1]
        taps = jnp.concatenate([k.astype(BF).reshape(192, 256) for k in (k0, k1, k2)], axis=1)
        return dot(taps, tdown_ref[...].reshape(768, 256)) + bias

    spread_out = [spatial(i) for i in range(2)]
    made = [temporal(s) for s in spread_out]
    for i in range(2):
        h2_ref[q + i] = silu(made[i]).astype(BF).reshape(6, 2, 16, 256)


def third(h2_ref, wout_ref, tout_ref, bias, masks):
    def spatial(q):
        taps = [h2_ref[q + a, b : b + 4].reshape(128, 256) for a in range(3) for b in range(3)]
        return dot(jnp.concatenate(taps, axis=1), wout_ref[...].reshape(2304, 256))

    def temporal(s):
        before = pltpu.roll(s, 1, 0).reshape(4, 2, 16, 256)
        s = s.reshape(4, 2, 16, 256)
        k0 = before * masks[0]
        k1 = jnp.concatenate([before[:, 1:2], s[:, 0:1]], axis=1) * masks[1]
        taps = jnp.concatenate([k.astype(BF).reshape(128, 256) for k in (k0, k1, s)], axis=1)
        return dot(taps, tout_ref[...].reshape(768, 256)) + bias

    made = [temporal(s) for s in [spatial(q) for q in range(2)]]
    return jnp.concatenate(made, axis=0).astype(BF)


OFFSETS = sorted(
    ((dx, dy) for dx in range(4) for dy in range(4) if dx or dy),
    key=lambda o: (-min(o[0], 4 - o[0]) - min(o[1], 4 - o[1]), o),
)


def kernel(
    clips,
    x_hbm, clip_hbm, owner_hbm, win_hbm, tin_hbm, bin_hbm, down_hbm, tdown_hbm, bdown_hbm, wout_hbm, tout_hbm, bout_hbm,
    landed,
    x_in, clip_ref, owner_ref, win_ref, tin_ref, bin_ref, down, tdown, bdown_ref, wout, tout, bout_ref,
    xpad, recv, perms, xs, w1, lt, wt, h1, h2, parts,
    load_sem, own_sem, send_sem, recv_sem, fsend_sem, frecv_sem, send2_sem, recv2_sem,
):
    me, row = lax.axis_index("tm"), lax.axis_index("tile")
    n, n_rows = lax.axis_size("tm"), lax.axis_size("tile")
    core = lax.rem(row, 2)
    at_top, at_bottom = row == 0, row == n_rows - 1
    barrier = pltpu.get_barrier_semaphore()

    def beside(dx, dy):
        return lax.rem(me // 4 + dx, 4) * 4 + lax.rem(lax.rem(me, 4) + dy, 4)

    for o in OFFSETS:
        pl.semaphore_signal(barrier, inc=1, device_id={"tm": beside(*o)}, device_id_type=MESH)

    @pl.when(jnp.logical_not(at_top))
    def _():
        pl.semaphore_signal(barrier, inc=1, device_id={"tile": row - 1}, device_id_type=MESH)

    @pl.when(jnp.logical_not(at_bottom))
    def _():
        pl.semaphore_signal(barrier, inc=1, device_id={"tile": row + 1}, device_id_type=MESH)

    x_load, *loads = [
        pltpu.make_async_copy(source, target, load_sem.at[i])
        for i, (source, target) in enumerate(
            (
                (x_hbm, x_in), (clip_hbm, clip_ref), (owner_hbm, owner_ref), (win_hbm, win_ref), (tin_hbm, tin_ref),
                (bin_hbm, bin_ref), (bdown_hbm, bdown_ref), (bout_hbm, bout_ref), (down_hbm, down),
                (tdown_hbm, tdown), (wout_hbm, wout), (tout_hbm, tout),
            )
        )
    ]
    x_load.start()
    for load in loads:
        load.start()
    x_load.wait()
    mine = jnp.concatenate([x_in[f].astype(F32) for f in range(4)], axis=0)
    side = jnp.zeros((16, 192), F32)
    xpad[...] = jnp.concatenate([side, mine, side], axis=1).astype(BF)
    loads[0].wait()
    loads[1].wait()
    w1[...] = jnp.zeros(w1.shape, BF)
    r, c = iota((256, 256), 0), iota((256, 256), 1)
    perms[0] = one_hot((r % 16) * 16 + ((r // 16) % 4) * 4 + r // 64, c)
    owner = jnp.zeros((8, 256), jnp.int32)
    for k in range(n):
        owner = owner + jnp.where(iota((8, 256), 1) % 16 == k, owner_ref[k], 0)
    spot = ((c // 16) % 2) * 8 + c // 32
    perms[1] = one_hot(r, owner[:1] * 16 + spot)
    same = clip_masks(clip_ref, clips)
    first_masks = [same(0, -2), same(0, -1), same(2, 0), same(2, 1)]
    pair_mask = jnp.stack([same(1, 0), same(3, 2)])

    def wide(one, two):
        both = jnp.stack([one, two])
        return jnp.concatenate([both, both], axis=2)

    second_masks = [wide(same(1, -1), same(3, 1)), wide(same(1, 0), same(3, 2))]
    third_masks = [wide(same(1, -3), same(3, -1)), wide(same(1, -1), same(3, 1))]
    pl.semaphore_wait(barrier, n - 1 + jnp.where(at_top, 0, 1) + jnp.where(at_bottom, 0, 1))

    def patch(who):
        return xpad.at[:, pl.ds(pl.multiple_of(who * STEP, 128), PATCH)]

    def across(i, o, source, target, send, recv_):
        to = beside(*o)
        return pltpu.make_async_remote_copy(
            src_ref=source(to), dst_ref=target(me), send_sem=send.at[i], recv_sem=recv_.at[me],
            device_id={"tm": to}, device_id_type=MESH,
        )

    def from_across(i, o, source, target, send, recv_):
        other = beside(-o[0] % 4, -o[1] % 4)
        return other, pltpu.make_async_remote_copy(
            src_ref=source(me), dst_ref=target(other), send_sem=send.at[i], recv_sem=recv_.at[other],
            device_id={"tm": other}, device_id_type=MESH,
        )

    out_way = (patch, lambda who: recv.at[1, who], send_sem, recv_sem)
    back_way = (lambda who: parts.at[who], lambda who: landed.at[who], send2_sem, recv2_sem)

    def passed(source, way):
        to = row + 1 - 2 * way
        return pltpu.make_async_remote_copy(
            src_ref=recv.at[1, source], dst_ref=recv.at[2 * way, source], send_sem=fsend_sem.at[way, source],
            recv_sem=frecv_sem.at[way, source], device_id={"tile": to}, device_id_type=MESH,
        )

    far_up, far_down = jnp.logical_and(core == 0, jnp.logical_not(at_top)), jnp.logical_and(core == 1, jnp.logical_not(at_bottom))

    def pass_on(source):
        @pl.when(jnp.logical_or(far_up, far_down))
        def _():
            passed(source, 1 - core).start()

        passed(source, core).start()

    for i, o in enumerate(OFFSETS):
        across(i, o, *out_way).start()
    own = pltpu.make_async_copy(patch(me), recv.at[1, me], own_sem)
    own.start()
    own.wait()
    pass_on(me)
    for load in loads[2:7]:
        load.wait()
    build_first_weights(win_ref, w1)
    build_temporal_weights(tin_ref, wt)
    bias_in, bias_down = bin_ref[...], bdown_ref[...]
    @pl.when(at_top)
    def _():
        recv[0] = jnp.zeros(recv.shape[1:], BF)

    @pl.when(at_bottom)
    def _():
        recv[2] = jnp.zeros(recv.shape[1:], BF)

    for i, o in enumerate(OFFSETS):
        other, copy = from_across(i, o, *out_way)
        copy.wait_recv()
        pass_on(other)
    for load in loads[7:]:
        load.wait()
    spread(recv, perms, xs, 1)

    def near(k, carry):
        passed(k, 1 - core).wait_recv()
        return carry

    lax.fori_loop(0, n, near, 0)
    spread(recv, perms, xs, 2 * (1 - core))

    def section_one(row0, rows):
        first_spatial(xs, w1, lt, first_masks, row0, rows)
        first_temporal(lt, wt, h1, bias_in, pair_mask, row0, rows)

    def clear_left_one():
        @pl.when(me == 0)
        def _():
            h1[1, :, :, :, :, :128] = jnp.zeros((9, 2, 2, 16, 128), BF)

    section_one(4 * (1 - core), 5)
    clear_left_one()
    second(h1, down, tdown, h2, bias_down, second_masks, 2 * (1 - core))

    @pl.when(jnp.logical_or(far_up, far_down))
    def _():
        def far(k, carry):
            passed(k, core).wait_recv()
            return carry

        lax.fori_loop(0, n, far, 0)

    spread(recv, perms, xs, 2 * core)
    section_one(5 * core, 4)
    clear_left_one()

    @pl.when(at_top)
    def _():
        h1[:, 2] = jnp.zeros((7, 2, 2, 16, 256), BF)

    second(h1, down, tdown, h2, bias_down, second_masks, 2 * core)

    @pl.when(at_top)
    def _():
        h2[0] = jnp.zeros((6, 2, 16, 256), BF)

    @pl.when(at_bottom)
    def _():
        h2[3] = jnp.zeros((6, 2, 16, 256), BF)

    @pl.when(me == 0)
    def _():
        h2[:, 0] = jnp.zeros((4, 2, 16, 256), BF)

    @pl.when(me == n - 1)
    def _():
        h2[:, 5] = jnp.zeros((4, 2, 16, 256), BF)

    encoded = third(h2, wout, tout, bout_ref[...], third_masks)
    parts[...] = dot(perms[1], encoded).astype(BF).reshape(16, 16, 256)
    for i, o in enumerate(OFFSETS):
        across(i, o, *back_way).start()
    own = pltpu.make_async_copy(parts.at[me], landed.at[me], own_sem)
    own.start()
    own.wait()
    for i, o in enumerate(OFFSETS):
        across(i, o, *out_way).wait_send()

    def settle(k, carry):
        passed(k, core).wait_send()
        return carry

    lax.fori_loop(0, n, settle, 0)

    @pl.when(jnp.logical_or(far_up, far_down))
    def _():
        def settle_far(k, carry):
            passed(k, 1 - core).wait_send()
            return carry

        lax.fori_loop(0, n, settle_far, 0)

    for i, o in enumerate(OFFSETS):
        across(i, o, *back_way).wait_send()
        from_across(i, o, *back_way)[1].wait_recv()


def lay_out(landed, out_ref):
    r, c = iota((256, 256), 0), iota((256, 256), 1)
    perm = one_hot(((r // 4) % 16) * 16 + (r // 64) * 4 + r % 4, c)
    out_ref[...] = dot(perm, landed[...].reshape(256, 256)).astype(BF).reshape(2, 2, 64, 256)


def per_device(
    haar_video, clip_lengths, block_owner, spatial_in, temporal_in, bias_in, spatial_down, temporal_down, bias_down,
    spatial_out, temporal_out, bias_out,
):
    clips = clip_lengths.shape[0]
    vmem, hbm = pl.BlockSpec(memory_space=pltpu.VMEM), pl.BlockSpec(memory_space=pl.ANY)
    dma = pltpu.SemaphoreType.DMA
    landed = pl.pallas_call(
        functools.partial(kernel, clips),
        out_shape=jax.ShapeDtypeStruct((16, 16, 256), BF),
        in_specs=[hbm] * 12,
        out_specs=hbm,
        scratch_shapes=[
            pltpu.VMEM(haar_video.shape, BF),
            pltpu.SMEM(clip_lengths.shape, jnp.int32),
            pltpu.SMEM(block_owner.shape, jnp.int32),
            pltpu.VMEM(spatial_in.shape, BF),
            pltpu.VMEM(temporal_in.shape, BF),
            pltpu.VMEM((1, 128), F32),
            pltpu.VMEM(spatial_down.shape, BF),
            pltpu.VMEM(temporal_down.shape, BF),
            pltpu.VMEM((1, 256), F32),
            pltpu.VMEM(spatial_out.shape, BF),
            pltpu.VMEM(temporal_out.shape, BF),
            pltpu.VMEM((1, 256), F32),
            pltpu.VMEM((16, 6528), BF),
            pltpu.VMEM((3, 16, 16, PATCH), BF),
            pltpu.VMEM((2, 256, 256), BF),
            pltpu.VMEM((12, 4, 16, PATCH), BF),
            pltpu.VMEM((5, 768, 384), BF),
            pltpu.VMEM((2, 13, 9, 2, 16, 256), BF),
            pltpu.VMEM((2, 256, 256), BF),
            pltpu.VMEM((7, 9, 2, 2, 16, 256), BF),
            pltpu.VMEM((4, 6, 2, 16, 256), BF),
            pltpu.VMEM((16, 16, 256), BF),
            dma((12,)),
            dma,
            dma((15,)),
            dma((16,)),
            dma((2, 16)),
            dma((2, 16)),
            dma((15,)),
            dma((16,)),
        ],
        compiler_params=pltpu.CompilerParams(
            collective_id=0, has_side_effects=True, vmem_limit_bytes=62 * 2**20
        ),
    )(
        haar_video, clip_lengths, block_owner, spatial_in, temporal_in, bias_in.reshape(1, 128), spatial_down,
        temporal_down, bias_down.reshape(1, 256), spatial_out, temporal_out, bias_out.reshape(1, 256),
    )
    return pl.pallas_call(
        lay_out,
        out_shape=jax.ShapeDtypeStruct((2, 2, 64, 256), BF),
        in_specs=[vmem],
        out_specs=vmem,
    )(landed)


def solution(mesh):
    placed = (P("tm", "tile", None), P(), P(), P(), P(), P(), P(), P(), P(), P(), P(), P())
    return jax.shard_map(
        per_device,
        mesh=mesh,
        in_specs=placed,
        out_specs=P("tm", "tile", None, None),
        check_vma=False,
    )
```
